256 devices in a mesh: dp: 4 (over x_hi, core), row: 8 (over x_lo, y), col: 8 (over z).
Axes of the slice: x: 4 (x_hi: 2, x_lo: 2; x = x_hi * 2 + x_lo), y: 4, z: 8, core: 2. Of those that a mesh axis runs over, the one named last changes fastest.
Arguments:
- tokens: bfloat16 [4096, 8192], P(('dp', 'row'), 'col'), may hold values from -6 to 6
- gate_pre: bfloat16 [4096, 14336], P(('dp', 'col'), 'row'), may hold values from -8 to 8
- up_pre: bfloat16 [4096, 14336], P(('dp', 'col'), 'row'), may hold values from -6 to 6
- d_hidden: bfloat16 [4096, 14336], P(('dp', 'col'), 'row'), may hold values from -6 to 6
- w_gate: bfloat16 [8192, 14336], P('col', 'row'), may hold values from -0.0625 to 0.0625
- w_up: bfloat16 [8192, 14336], P('col', 'row'), may hold values from -0.0625 to 0.0625
Outputs:
- d_tokens: bfloat16 [4096, 8192], P(('dp', 'row'), 'col')
- score_gate: float32 [8, 4, 256, 14336], P('col', 'dp', None, 'row')
- score_up: float32 [8, 4, 256, 14336], P('col', 'dp', None, 'row')
The draws below stay inside these ranges and needn't reach their ends.
All inputs are finite; a program needn't handle non-finite values.
Results may differ from the reference program's by a relative error of at most 0.0049.
Values may be sent and summed in bfloat16 or wider, within the bound.
No kernel may reach another device: no remote copies, remote signals or barrier semaphores. Data moves between devices by JAX's collectives and lax.ppermute only.
A program may use at most 128 MiB of HBM per device.

```python
import jax
import jax.numpy as jnp
from jax import lax

D = 8192
FFW = 14336
TOKENS = 4096
N_DP = 4
N_COL = 8


def level_of(own_key, extent, split, smallest, largest):
    gain = 1.0
    for position, parts in split:
        heights = jax.random.uniform(jax.random.fold_in(jax.random.fold_in(own_key, 6), position), (parts,), jnp.float32, smallest / len(split), largest / len(split))
        gain = gain * jnp.repeat(jnp.exp(heights), extent[position] // parts).reshape((-1,) + (1,) * (len(extent) - 1 - position))
    return gain


def noise(rng, extent, spread, bound, cuts=(), dtype=jnp.bfloat16):
    values = spread * jax.random.normal(rng, extent, jnp.float32)
    if cuts:
        values = values * level_of(rng, extent, cuts, -0.22, 0.18)
    return jnp.clip(values, -bound, bound).astype(dtype)


def setup_inputs(seed: int = 0) -> dict:
    seeds = jax.random.split(jax.random.key(seed), 7)
    return {
        "tokens": noise(seeds[0], (TOKENS, D), 1.0, 6.0, ((0, 32), (1, 8))),
        "gate_pre": noise(seeds[1], (TOKENS, FFW), 1.5, 8.0, ((0, 32), (1, 8))),
        "up_pre": noise(seeds[2], (TOKENS, FFW), 1.0, 6.0, ((0, 32), (1, 8))),
        "d_hidden": noise(seeds[3], (TOKENS, FFW), 1.0, 6.0, ((0, 32), (1, 8))),
        "w_gate": noise(seeds[4], (D, FFW), D ** -0.5, 0.0625, ((0, 8), (1, 8))),
        "w_up": noise(seeds[5], (D, FFW), D ** -0.5, 0.0625, ((0, 8), (1, 8))),
    }


def reference(tokens, gate_pre, up_pre, d_hidden, w_gate, w_up):
    gate_value = gate_pre.astype(jnp.float32)
    up_value = up_pre.astype(jnp.float32)
    upstream = d_hidden.astype(jnp.float32)
    logistic = jax.nn.sigmoid(gate_value)
    grad_up = (upstream * gate_value * logistic).astype(jnp.bfloat16)
    grad_gate = (upstream * up_value * logistic * (1.0 + gate_value * (1.0 - logistic))).astype(jnp.bfloat16)
    contract_cols = (((1,), (1,)), ((), ()))
    d_tokens = lax.dot_general(grad_gate, w_gate, contract_cols, preferred_element_type=jnp.float32)
    d_tokens = d_tokens + lax.dot_general(grad_up, w_up, contract_cols, preferred_element_type=jnp.float32)
    d_tokens = d_tokens.astype(jnp.bfloat16)
    weight_gate = jnp.dot(tokens.T, grad_gate, preferred_element_type=jnp.float32)
    score_gate = (-w_gate.astype(jnp.float32) * weight_gate).reshape(N_COL, N_DP, D // (N_COL * N_DP), FFW)
    weight_up = jnp.dot(tokens.T, grad_up, preferred_element_type=jnp.float32)
    score_up = (-w_up.astype(jnp.float32) * weight_up).reshape(N_COL, N_DP, D // (N_COL * N_DP), FFW)
    return (d_tokens, score_gate, score_up)
```

```python
import jax
import jax.numpy as jnp
from jax import lax
from jax.sharding import PartitionSpec as P

F32 = jnp.float32
BF16 = jnp.bfloat16
UNIT = 14
GROUPS = ((4, False), (4, False), (3, True), (3, True))


def around(value):
    perm = []
    for dp in range(4):
        step = 1 if dp % 2 == 0 else -1
        for z in range(8):
            perm.append((dp * 8 + z, dp * 8 + (z + step) % 8))
    return lax.ppermute(value, ("dp", "col"), perm)


def swap_core(value):
    return lax.ppermute(value, "dp", [(i, i ^ 1) for i in range(4)])


def swap_chip(value):
    return lax.ppermute(value, "dp", [(i, i ^ 2) for i in range(4)])


def swap_pair(value):
    return lax.ppermute(value, "row", [(i, i ^ 4) for i in range(8)])


def along_y(value, step):
    return lax.ppermute(
        value, "row", [(i, (i // 4) * 4 + (i % 4 + step) % 4) for i in range(8)]
    )


def pick(blocks, index):
    return lax.dynamic_index_in_dim(blocks, index, 0, keepdims=False)


def hidden_grads(gate_pre, up_pre, d_hidden):
    gate_value = gate_pre.astype(F32)
    up_value = up_pre.astype(F32)
    upstream = d_hidden.astype(F32)
    logistic = jax.nn.sigmoid(gate_value)
    grad_up = (upstream * gate_value * logistic).astype(BF16)
    grad_gate = (upstream * up_value * logistic * (1.0 + gate_value * (1.0 - logistic))).astype(
        BF16
    )
    return jnp.concatenate([grad_gate, grad_up], 1)


def shards(tokens, gate_pre, up_pre, d_hidden, w_gate, w_up):
    rows, width = tokens.shape
    hidden = gate_pre.shape[1]
    slab = width // 4
    half = rows // 2
    replica = lax.axis_index("dp")
    core = lax.rem(replica, 2)
    sign = 1 - 2 * core
    row = lax.axis_index("row")
    pair, y = row // 4, lax.rem(row, 4)
    col = lax.axis_index("col")

    def wrap(v):
        return lax.rem(v + 32, 8)

    bounds, at = [], 0
    for parts, _ in GROUPS:
        size = hidden * parts // UNIT
        bounds.append((at, at + size))
        at += size

    own, other = [], []
    for lo, hi in bounds:
        g = hidden_grads(gate_pre[:, lo:hi], up_pre[:, lo:hi], d_hidden[:, lo:hi])
        own.append(g)
        other.append(swap_core(g))

    def gather(g, o):
        n = g.shape[0]
        first = around(jnp.concatenate([g, o], 0))
        second = around(first)
        third = around(second)
        last = around(third[:n])
        return jnp.concatenate([g, first, second, third, last], 0)

    mate = swap_pair(tokens)
    both = jnp.where(pair == 0, jnp.stack([tokens, mate]), jnp.stack([mate, tokens]))
    from_below = along_y(both, 1)
    from_above = along_y(both, -1)
    from_far = along_y(both, 2)
    near = jnp.concatenate([both, from_above, from_far, from_below], 0)
    rel = []
    for s in range(8):
        ident = wrap(col - sign * s)
        rel.append(pick(near, lax.rem(lax.rem(ident, 4) - y + 4, 4) * 2 + ident // 4))
    lent = swap_core(jnp.concatenate([rel[7], rel[6], rel[5]], 0))
    lent = [lent[i * rows : (i + 1) * rows] for i in range(3)]
    pieces = [rel[0], rel[1], lent[0], rel[2], lent[1], rel[3], lent[2], rel[4]]
    order = [replica, replica ^ 2, replica ^ 1, replica ^ 3]

    def transposed(parts):
        x = jnp.concatenate(parts, 0)
        return jnp.concatenate(
            [lax.dynamic_slice_in_dim(x, q * slab, slab, 1).T for q in order], 0
        )

    xt = transposed(pieces)
    xt_halves = [
        transposed([p[:half] for p in pieces]),
        transposed([p[half:] for p in pieces]),
    ]

    def mm(a, b):
        return lax.dot_general(a, b, (((1,), (0,)), ((), ())), preferred_element_type=F32)

    def mm_t(a, b):
        return lax.dot_general(a, b, (((1,), (1,)), ((), ())), preferred_element_type=F32)

    def weights(lo, hi):
        return jnp.concatenate([w_gate[:, lo:hi], w_up[:, lo:hi]], 1)

    def score(part_send, part_keep, lo, hi):
        got = swap_core(part_send)
        kept = part_keep + got.astype(F32)
        far = swap_chip(kept[slab:].astype(BF16))
        total = kept[:slab] + far.astype(F32)
        size = hi - lo
        gate_slab = lax.dynamic_slice(w_gate, (replica * slab, lo), (slab, size)).astype(F32)
        up_slab = lax.dynamic_slice(w_up, (replica * slab, lo), (slab, size)).astype(F32)
        return -gate_slab * total[:, :size], -up_slab * total[:, size:]

    gate_scores, up_scores = [None] * len(GROUPS), [None] * len(GROUPS)
    d_full = None
    for k, (_, split) in enumerate(GROUPS):
        if split:
            continue
        lo, hi = bounds[k]
        grads = gather(own[k], other[k])
        d_part = mm_t(grads, weights(lo, hi))
        d_full = d_part if d_full is None else d_full + d_part
        part_send = mm(xt[2 * slab :], grads).astype(BF16)
        part_keep = mm(xt[: 2 * slab], grads)
        gate_scores[k], up_scores[k] = score(part_send, part_keep, lo, hi)

    d_full = d_full.reshape(8, 2, half, width)
    outs = []
    held = {}
    for h in range(2):
        total = d_full[:, h].reshape(8 * half, width)
        for k, (_, split) in enumerate(GROUPS):
            if not split:
                continue
            lo, hi = bounds[k]
            cut = slice(h * half, (h + 1) * half)
            grads = gather(own[k][cut], other[k][cut])
            total = total + mm_t(grads, weights(lo, hi))
            x = xt_halves[h]
            send = mm(x[2 * slab :], grads)
            keep = mm(x[: 2 * slab], grads)
            if h == 0:
                held[k] = (send, keep)
            else:
                gate_scores[k], up_scores[k] = score(
                    (held[k][0] + send).astype(BF16), held[k][1] + keep, lo, hi
                )
        total = total.reshape(8, half, width)
        back = swap_core(jnp.stack([total[2], total[4], total[6]]).astype(BF16)).astype(F32)
        arranged = jnp.stack(
            [total[0], total[1], total[3], total[5], total[7], back[2], back[1], back[0]]
        )

        def at_y(step):
            yy = lax.rem(y + step + 4, 4)
            return jnp.stack(
                [pick(arranged, wrap(sign * (col - (xl * 4 + yy)))) for xl in range(2)]
            )

        up = along_y(at_y(1).astype(BF16), 1)
        down = along_y(at_y(-1).astype(BF16), -1)
        far = along_y(at_y(2).astype(BF16), 2)
        summed = at_y(0) + up.astype(F32) + down.astype(F32) + far.astype(F32)
        sent = swap_pair(pick(summed, 1 - pair).astype(BF16))
        outs.append((pick(summed, pair) + sent.astype(F32)).astype(BF16))

    d_tokens = jnp.concatenate(outs, 0)
    score_gate = jnp.concatenate(gate_scores, 1).reshape(1, 1, slab, hidden)
    score_up = jnp.concatenate(up_scores, 1).reshape(1, 1, slab, hidden)
    return (d_tokens, score_gate, score_up)


def solution(mesh):
    placed = (
        P(("dp", "row"), "col"),
        P(("dp", "col"), "row"),
        P(("dp", "col"), "row"),
        P(("dp", "col"), "row"),
        P("col", "row"),
        P("col", "row"),
    )
    return jax.shard_map(
        shards,
        mesh=mesh,
        in_specs=placed,
        out_specs=(
            P(("dp", "row"), "col"),
            P("col", "dp", None, "row"),
            P("col", "dp", None, "row"),
        ),
        check_vma=False,
    )
```

```python
import functools

import jax
import jax.numpy as jnp
from jax import lax
from jax.experimental import pallas as pl
from jax.experimental.pallas import tpu as pltpu
from jax.sharding import PartitionSpec as P

F32 = jnp.float32
BF16 = jnp.bfloat16
GROUPS = (4, 4, 3, 3)
FIRST_ROWS = 80
TILE = 256
VMEM = pl.BlockSpec(memory_space=pltpu.VMEM)
ANY = pl.BlockSpec(memory_space=pl.ANY)
MINE = (0, 1, 3, 5, 7)
LENT = (2, 4, 6)


def around(value, cross=False):
    perm = []
    for dp in range(4):
        to = dp ^ 1 if cross else dp
        step = 1 if to % 2 == 0 else -1
        for z in range(8):
            perm.append((dp * 8 + z, to * 8 + (z + step) % 8))
    return lax.ppermute(value, ("dp", "col"), perm)


def swap_core(value):
    return lax.ppermute(value, "dp", [(i, i ^ 1) for i in range(4)])


def swap_chip(value):
    return lax.ppermute(value, "dp", [(i, i ^ 2) for i in range(4)])


def swap_pair(value):
    return lax.ppermute(value, "row", [(i, i ^ 4) for i in range(8)])


def along_y(value, step):
    return lax.ppermute(
        value, "row", [(i, (i // 4) * 4 + (i % 4 + step) % 4) for i in range(8)]
    )


def place():
    replica = lax.axis_index("dp")
    row = lax.axis_index("row")
    col = lax.axis_index("col")
    sign = 1 - 2 * lax.rem(replica, 2)
    return replica, row // 4, lax.rem(row, 4), col, sign


def wrap(v, n=8):
    return lax.rem(v + 8 * n, n)


def run(kernel, outs, ins, after=(), scratch=(), limit=None, flops=0, moved=0, alias=None):
    count = len(ins)
    waits = len(after)

    def body(*refs):
        kernel(*refs[:count], *refs[count + waits :])

    return pl.pallas_call(
        body,
        out_shape=[jax.ShapeDtypeStruct(shape, dtype) for shape, dtype, _ in outs],
        in_specs=[spec for _, spec in ins] + [ANY] * waits,
        out_specs=[spec for _, _, spec in outs],
        scratch_shapes=list(scratch),
        input_output_aliases=alias or {},
        compiler_params=pltpu.CompilerParams(vmem_limit_bytes=limit) if limit else None,
        cost_estimate=pl.CostEstimate(flops=flops, bytes_accessed=moved, transcendentals=0),
    )(*[a for a, _ in ins], *after)


def nt(a, b):
    return lax.dot_general(a, b, (((1,), (1,)), ((), ())), preferred_element_type=F32)


def grads_of(gate, up, flow, out):
    size = gate.shape[1]
    gate_value = gate[...].astype(F32)
    flow_value = flow[...].astype(F32)
    logistic = jax.nn.sigmoid(gate_value)
    weighted = flow_value * logistic
    out[:, size:] = (weighted * gate_value).astype(BF16)
    out[:, :size] = (
        weighted * up[...].astype(F32) * (1.0 + gate_value * (1.0 - logistic))
    ).astype(BF16)


def grads_kernel(row, lo, gate_any, up_any, flow_any, out, gate, up, flow, sems):
    rows, size = gate.shape
    copies = [
        pltpu.make_async_copy(source.at[pl.ds(row, rows), pl.ds(lo, size)], target, sems.at[i])
        for i, (source, target) in enumerate(((gate_any, gate), (up_any, up), (flow_any, flow)))
    ]
    for copy in copies:
        copy.start()
    for copy in copies:
        copy.wait()
    grads_of(gate, up, flow, out)


def join_kernel(a, b, out):
    n = a.shape[0]
    out[:n] = a[...]
    out[n:] = b[...]


def pick_near(refs, ident, pair, y, write):
    k = wrap(lax.rem(ident, 4) - y, 4)
    j = lax.rem(ident // 4 + pair, 2)
    for i, ref in enumerate(refs):

        @pl.when(k == i)
        def _():
            write(ref[j])


def lend_tokens_kernel(near0, near1, near2, near3, out):
    _, pair, y, col, sign = place()
    for i in range(3):

        def write(value, i=i):
            out[i] = value

        pick_near((near0, near1, near2, near3), wrap(col - sign * (7 - i)), pair, y, write)


def tokens_kernel(cut, near0, near1, near2, near3, got, out, laid):
    replica, pair, y, col, sign = place()
    rows, width = near0.shape[1:]
    slab = width // 4
    rest = rows - cut

    def put(at, value):
        laid[at * cut : (at + 1) * cut] = value[:cut]
        laid[8 * cut + at * rest : 8 * cut + (at + 1) * rest] = value[cut:]

    for s, at in enumerate(MINE):
        pick_near(
            (near0, near1, near2, near3),
            wrap(col - sign * s),
            pair,
            y,
            functools.partial(put, at),
        )
    for i, at in enumerate(LENT):
        put(at, got[i])
    for i, flip in enumerate((0, 2, 1, 3)):
        q = replica ^ flip
        columns = pl.ds(pl.multiple_of(q * slab, slab), slab)
        for t in range(0, 8 * rows, TILE):
            out[i * slab : (i + 1) * slab, t : t + TILE] = laid[t : t + TILE, columns].T


def lay(pieces, cut, out, base, column, size):
    own, first, second, third, last = pieces
    n = own.shape[0]
    rest = n - cut
    blocks = [(own, 0), (first, 0), (first, n), (second, 0), (second, n), (third, 0), (third, n), (last, 0)]
    for at, (ref, start) in enumerate(blocks):
        out[base + at * cut : base + (at + 1) * cut, column : column + size] = ref[start : start + cut]
        if rest:
            begin = base + 8 * cut + at * rest
            out[begin : begin + rest, column : column + size] = ref[start + cut : start + n]


def weight_kernel(cut, own, first, second, third, last, xt, cat, send, keep):
    lay((own, first, second, third, last), cut, cat, 0, 0, own.shape[1])
    half = xt.shape[0] // 2

    @pl.loop(0, cat.shape[1] // TILE)
    def _(t):
        columns = pl.ds(pl.multiple_of(t * TILE, TILE), TILE)
        grads = cat[:, columns]
        send[:, columns] = jnp.dot(xt[half:], grads, preferred_element_type=F32).astype(BF16)
        keep[:, columns] = jnp.dot(xt[:half], grads, preferred_element_type=F32)


def weight_tail_kernel(at, own, first, second, third, last, early, xt, cat, send, keep, full):
    size = own.shape[1] // 2
    span = early.shape[1] // 2
    head = early.shape[0]
    n = own.shape[0]
    lay((own, first, second, third, last), n, cat, 0, 0, 2 * size)
    half = xt.shape[0] // 2
    for part in range(2):
        full[:head] = early[:, part * span + at : part * span + at + size]
        full[head:] = cat[:, part * size : (part + 1) * size]
        columns = slice(part * size, (part + 1) * size)
        grads = full[...]
        send[:, columns] = jnp.dot(xt[half:], grads, preferred_element_type=F32).astype(BF16)
        keep[:, columns] = jnp.dot(xt[:half], grads, preferred_element_type=F32)


def pair_kernel(keep, got, near, far):
    slab = keep.shape[0] // 2
    near[...] = keep[:slab] + got[:slab].astype(F32)
    far[...] = (keep[slab:] + got[slab:].astype(F32)).astype(BF16)


def score_kernel(lo, aliased, near, far, w_gate, w_up, *refs):
    out_gate, out_up, slab_gate, slab_up, res_gate, res_up, sems = refs[2 if aliased else 0 :]
    replica = lax.axis_index("dp")
    slab, size = slab_gate.shape
    rows = pl.ds(pl.multiple_of(replica * slab, slab), slab)
    read = [
        pltpu.make_async_copy(w.at[rows, pl.ds(lo, size)], target, sems.at[i])
        for i, (w, target) in enumerate(((w_gate, slab_gate), (w_up, slab_up)))
    ]
    write = [
        pltpu.make_async_copy(value, out.at[:, pl.ds(lo, size)], sems.at[2 + i])
        for i, (value, out) in enumerate(((res_gate, out_gate), (res_up, out_up)))
    ]
    for copy in read:
        copy.start()
    for i, (w, value) in enumerate(((slab_gate, res_gate), (slab_up, res_up))):
        read[i].wait()
        columns = slice(i * size, (i + 1) * size)
        value[...] = -w[...].astype(F32) * (near[:, columns] + far[:, columns].astype(F32))
        write[i].start()
    for copy in write:
        copy.wait()


def split_lent(total, t, r, mine, lend, columns):
    for i, at in enumerate(MINE):
        mine[i * r : (i + 1) * r, columns] = total[at * r : (at + 1) * r]
    for i, at in enumerate(LENT):
        lend[i * r : (i + 1) * r, columns] = total[at * r : (at + 1) * r].astype(BF16)


def start_weights(w_gate, w_up, gate, up, sems, lo=0):
    size = gate.shape[1]
    copies = []
    for t in range(gate.shape[0] // TILE):
        rows = pl.ds(t * TILE, TILE)
        copies.append(
            [
                pltpu.make_async_copy(w.at[rows, pl.ds(lo, size)], target.at[rows], sems.at[t, i])
                for i, (w, target) in enumerate(((w_gate, gate), (w_up, up)))
            ]
        )
    for copy in copies:
        copy[0].start()
        copy[1].start()
    return copies


def tokens_early_kernel(
    bounds, own, first, second, third, last, cat0, cat1, w_gate, w_up, cat, mine, lend, gate, up, sems
):
    r = own.shape[0]
    size = own.shape[1] // 2
    copies = start_weights(w_gate, w_up, gate, up, sems)
    lay((own, first, second, third, last), r, cat, 0, 0, 2 * size)
    for t in range(gate.shape[0] // TILE):
        for copy in copies[t]:
            copy.wait()
        rows = slice(t * TILE, (t + 1) * TILE)
        total = None
        for ref, (lo, hi) in zip((cat0, cat1, cat), bounds):
            for i, w in enumerate((gate, up)):
                width = hi - lo
                term = nt(ref[: 8 * r, i * width : (i + 1) * width], w[rows, lo:hi])
                total = term if total is None else total + term
        split_lent(total, t, r, mine, lend, rows)


def tokens_part_kernel(bounds, r, cat0, cat1, w_gate, w_up, out, gate, up, sems):
    copies = start_weights(w_gate, w_up, gate, up, sems)
    for t in range(gate.shape[0] // TILE):
        for copy in copies[t]:
            copy.wait()
        rows = slice(t * TILE, (t + 1) * TILE)
        total = None
        for ref, (lo, hi) in zip((cat0, cat1), bounds):
            width = hi - lo
            for i, w in enumerate((gate, up)):
                term = nt(ref[-8 * r :, i * width : (i + 1) * width], w[rows, lo:hi])
                total = term if total is None else total + term
        out[:, rows] = total


def tokens_late_kernel(
    lo, r, own, first, second, third, last, part, cat0, w_gate, w_up, mine, lend, cat, gate, up, sems
):
    copies = start_weights(w_gate, w_up, gate, up, sems, lo)
    size = own.shape[1] // 2
    lay((own, first, second, third, last), r, cat, 0, 0, 2 * size)
    for t in range(gate.shape[0] // TILE):
        for copy in copies[t]:
            copy.wait()
        rows = slice(t * TILE, (t + 1) * TILE)
        total = part[:, rows]
        begin = 0
        for ref in (cat0, cat):
            width = ref.shape[1] // 2
            for i, w in enumerate((gate, up)):
                total = total + nt(
                    ref[:, i * width : (i + 1) * width], w[rows, begin : begin + width]
                )
            begin += width
        split_lent(total, t, r, mine, lend, rows)


def spread_kernel(mine, back, up, down, far, hold, every):
    _, pair, y, col, sign = place()
    r = every.shape[1]
    for s in range(5):
        every[s] = mine[s * r : (s + 1) * r]
    for i in range(3):
        every[7 - i] = back[i * r : (i + 1) * r].astype(F32)
    for out, step in ((up, 1), (down, 3), (far, 2), (hold, 0)):
        for j in range(2):
            ident = lax.rem(pair + j, 2) * 4 + lax.rem(y + step, 4)
            out[j] = every[wrap(sign * (col - ident))].astype(out.dtype)


def sum_y_kernel(hold, up, down, far, own, send):
    def total(j):
        return hold[j] + up[j].astype(F32) + (down[j].astype(F32) + far[j].astype(F32))

    own[...] = total(0)
    send[...] = total(1).astype(BF16)


def last_kernel(own, got, out):
    out[...] = (own[...] + got[...].astype(F32)).astype(BF16)


def last_join_kernel(own, got, before, out):
    cut = before.shape[0]
    out[:cut] = before[...]
    out[cut:] = (own[...] + got[...].astype(F32)).astype(BF16)


def shards(tokens, gate_pre, up_pre, d_hidden, w_gate, w_up):
    rows, width = tokens.shape
    hidden = gate_pre.shape[1]
    slab = width // 4
    cut = FIRST_ROWS
    rest = rows - cut
    many = 8 * rows
    mib = 1 << 20
    bounds, at = [], 0
    for parts in GROUPS:
        size = hidden * parts // sum(GROUPS)
        bounds.append((at, at + size))
        at += size

    def v(*arrays):
        return [(a, VMEM) for a in arrays]

    def grads(row, n, lo, hi, after=()):
        size = hi - lo
        return run(
            functools.partial(grads_kernel, row, lo),
            [((n, 2 * size), BF16, VMEM)],
            [(gate_pre, ANY), (up_pre, ANY), (d_hidden, ANY)],
            after,
            [pltpu.VMEM((n, size), BF16)] * 3 + [pltpu.SemaphoreType.DMA((3,))],
            flops=20 * n * size,
            moved=10 * n * size,
        )[0]

    def join(a, b, after=()):
        shape = (2 * a.shape[0],) + a.shape[1:]
        return run(
            join_kernel, [(shape, a.dtype, VMEM)], v(a, b), after, moved=4 * a.size
        )[0]

    def ring(g, after=()):
        first = join(around(g), around(g, True), after)
        second = around(first)
        third = around(second)
        last = around(third[: g.shape[0]])
        return (g, first, second, third, last)

    def weight_grads(pieces, xt, after):
        cols = pieces[0].shape[1]
        return run(
            functools.partial(weight_kernel, cut),
            [
                ((many, cols), BF16, VMEM),
                ((2 * slab, cols), BF16, VMEM),
                ((2 * slab, cols), F32, VMEM),
            ],
            v(*pieces, xt),
            after,
            limit=24 * mib,
            flops=2 * many * width * cols,
            moved=2 * many * (cols + width),
        )

    def weight_grads_tail(pieces, early, xt, column, after):
        cols = pieces[0].shape[1]
        return run(
            functools.partial(weight_tail_kernel, column),
            [
                ((8 * rest, cols), BF16, VMEM),
                ((2 * slab, cols), BF16, VMEM),
                ((2 * slab, cols), F32, VMEM),
            ],
            v(*pieces, early, xt),
            after,
            [pltpu.VMEM((many, cols // 2), BF16)],
            limit=24 * mib,
            flops=2 * many * width * cols,
            moved=2 * many * (cols + width),
        )

    def pair_sum(keep, send, after=()):
        cols = keep.shape[1]
        near, far = run(
            pair_kernel,
            [((slab, cols), F32, VMEM), ((slab, cols), BF16, VMEM)],
            v(keep, swap_core(send)),
            after,
            limit=16 * mib,
            moved=8 * keep.size,
        )
        return near, swap_chip(far)

    def scores(near, far, lo, hi, before, after=()):
        size = hi - lo
        shape = ((slab, hidden), F32, ANY)
        return run(
            functools.partial(score_kernel, lo, bool(before)),
            [shape, shape],
            v(near, far) + [(w_gate, ANY), (w_up, ANY)] + [(b, ANY) for b in before],
            after,
            [pltpu.VMEM((slab, size), BF16)] * 2
            + [pltpu.VMEM((slab, size), F32)] * 2
            + [pltpu.SemaphoreType.DMA((4,))],
            limit=16 * mib,
            moved=20 * slab * size,
            alias={4: 0, 5: 1} if before else None,
        )

    def weight_scratch(size):
        return [pltpu.VMEM((width, size), BF16)] * 2 + [
            pltpu.SemaphoreType.DMA((width // TILE, 2))
        ]

    def reduce_tokens(mine, lend, r, before=None, after=()):
        shape = (2, r, width)
        up, down, far, hold = run(
            spread_kernel,
            [(shape, BF16, VMEM)] * 3 + [(shape, F32, VMEM)],
            v(mine, swap_core(lend)),
            after,
            [pltpu.VMEM((8, r, width), F32)],
            limit=16 * mib,
            moved=40 * r * width,
        )
        own, send = run(
            sum_y_kernel,
            [((r, width), F32, VMEM), ((r, width), BF16, VMEM)],
            v(hold, along_y(up, 1), along_y(down, -1), along_y(far, 2)),
            limit=16 * mib,
            moved=26 * r * width,
        )
        got = swap_pair(send)
        if before is None:
            return run(
                last_kernel, [((r, width), BF16, VMEM)], v(own, got), moved=8 * r * width
            )[0]
        return run(
            last_join_kernel,
            [((rows, width), BF16, VMEM)],
            v(own, got, before),
            moved=8 * r * width,
        )[0]

    base, top = bounds[2][0], bounds[3][1]

    g0 = grads(0, rows, *bounds[0])
    both = join(tokens[None], swap_pair(tokens)[None], (g0,))
    unit0 = ring(g0)
    near = (both, along_y(both, -1), along_y(both, 2), along_y(both, 1))
    g1 = grads(0, rows, *bounds[1], (unit0[1],))
    unit1 = ring(g1)
    lend = run(
        lend_tokens_kernel, [((3, rows, width), BF16, VMEM)], v(*near), moved=12 * rows * width
    )[0]
    xt = run(
        functools.partial(tokens_kernel, cut),
        [((width, many), BF16, VMEM)],
        v(*near, swap_core(lend)),
        scratch=[pltpu.VMEM((many, width), BF16)],
        limit=24 * mib,
        moved=32 * rows * width,
    )[0]

    g2 = grads(0, cut, base, top, (unit0[4],))
    unit2 = ring(g2)
    cat0, send0, keep0 = weight_grads(unit0, xt, (g2,))
    near0, far0 = pair_sum(keep0, send0)

    g3 = grads(cut, rest, *bounds[2], (unit1[4],))
    unit3 = ring(g3)
    cat1, send1, keep1 = weight_grads(unit1, xt, (g3, near0))
    near1, far1 = pair_sum(keep1, send1)
    part = run(
        functools.partial(tokens_part_kernel, bounds[:2], rest),
        [((8 * rest, width), F32, VMEM)],
        v(cat0, cat1) + [(w_gate, ANY), (w_up, ANY)],
        (near1,),
        weight_scratch(base),
        limit=24 * mib,
        flops=4 * 8 * rest * width * base,
        moved=4 * width * base,
    )[0]
    done = scores(near0, far0, *bounds[0], (), (part,))

    g4 = grads(cut, rest, *bounds[3], (unit2[4],))
    unit4 = ring(g4)
    cat2, mine, lend = run(
        functools.partial(tokens_early_kernel, bounds[:2] + [(base, top)]),
        [
            ((8 * cut, 2 * (top - base)), BF16, VMEM),
            ((5 * cut, width), F32, VMEM),
            ((3 * cut, width), BF16, VMEM),
        ],
        v(*unit2, cat0, cat1) + [(w_gate, ANY), (w_up, ANY)],
        (g4, near1),
        weight_scratch(hidden),
        limit=32 * mib,
        flops=4 * 8 * cut * width * hidden,
        moved=4 * width * hidden,
    )
    d_early = reduce_tokens(mine, lend, cut)

    cat3, send3, keep3 = weight_grads_tail(unit3, cat2, xt, 0, (mine,))
    near3, far3 = pair_sum(keep3, send3)
    done = scores(near1, far1, *bounds[1], done, (near3,))

    mine, lend = run(
        functools.partial(tokens_late_kernel, base, rest),
        [((5 * rest, width), F32, VMEM), ((3 * rest, width), BF16, VMEM)],
        v(*unit4, part, cat3) + [(w_gate, ANY), (w_up, ANY)],
        (near3,),
        [pltpu.VMEM((8 * rest, 2 * (bounds[3][1] - bounds[3][0])), BF16)]
        + weight_scratch(top - base),
        limit=24 * mib,
        flops=4 * 8 * rest * width * (top - base),
        moved=4 * width * (top - base),
    )
    _, send4, keep4 = weight_grads_tail(
        unit4, cat2, xt, bounds[3][0] - base, (mine,)
    )
    d_tokens = reduce_tokens(mine, lend, rest, d_early)
    near4, far4 = pair_sum(keep4, send4)
    done = scores(near3, far3, *bounds[2], done)
    done = scores(near4, far4, *bounds[3], done)
    score_gate, score_up = [d.reshape(1, 1, slab, hidden) for d in done]
    return (d_tokens, score_gate, score_up)


def solution(mesh):
    placed = (
        P(("dp", "row"), "col"),
        P(("dp", "col"), "row"),
        P(("dp", "col"), "row"),
        P(("dp", "col"), "row"),
        P("col", "row"),
        P("col", "row"),
    )
    return jax.shard_map(
        shards,
        mesh=mesh,
        in_specs=placed,
        out_specs=(
            P(("dp", "row"), "col"),
            P("col", "dp", None, "row"),
            P("col", "dp", None, "row"),
        ),
        check_vma=False,
    )
```

```python
import functools

import jax
import jax.numpy as jnp
from jax import lax
from jax.experimental import pallas as pl
from jax.experimental.pallas import tpu as pltpu
from jax.sharding import PartitionSpec as P

F32 = jnp.float32
BF16 = jnp.bfloat16
GROUPS = (4, 6, 4)
FIRST_ROWS = 96
TILE = 256
SCALE = 1000000000
VMEM = pl.BlockSpec(memory_space=pltpu.VMEM)
ANY = pl.BlockSpec(memory_space=pl.ANY)
MINE = (0, 1, 3, 5, 7)
LENT = (2, 4, 6)


def around(value):
    perm = []
    for dp in range(4):
        step = 1 if dp % 2 == 0 else -1
        for z in range(8):
            perm.append((dp * 8 + z, dp * 8 + (z + step) % 8))
    return lax.ppermute(value, ("dp", "col"), perm)


def swap_core(value):
    return lax.ppermute(value, "dp", [(i, i ^ 1) for i in range(4)])


def swap_chip(value):
    return lax.ppermute(value, "dp", [(i, i ^ 2) for i in range(4)])


def swap_pair(value):
    return lax.ppermute(value, "row", [(i, i ^ 4) for i in range(8)])


def along_y(value, step):
    return lax.ppermute(
        value, "row", [(i, (i // 4) * 4 + (i % 4 + step) % 4) for i in range(8)]
    )


def place():
    col = lax.axis_index("col")
    sign = 1 - 2 * lax.rem(lax.axis_index("dp"), 2)
    return col, sign


def wrap(v, n=8):
    return lax.rem(v + 8 * n, n)


class Order:
    def __init__(self):
        self.before = ()

    def __call__(self, kernel, outs, ins, scratch=(), limit=None, alias=None, work=0.3):
        count, waits = len(ins), len(self.before)

        def body(*refs):
            kernel(*refs[:count], *refs[count + waits :])

        got = pl.pallas_call(
            body,
            out_shape=[make(shape, dtype) for make, shape, dtype, _ in outs],
            in_specs=[spec for _, spec in ins] + [ANY] * waits,
            out_specs=[spec for _, _, _, spec in outs],
            scratch_shapes=list(scratch),
            input_output_aliases=alias or {},
            compiler_params=pltpu.CompilerParams(vmem_limit_bytes=limit),
            cost_estimate=pl.CostEstimate(
                flops=int(work * SCALE), bytes_accessed=1, transcendentals=0
            ),
        )(*[a for a, _ in ins], *self.before)
        self.before = (got[-1],)
        return got


def mm(a, b):
    return jnp.dot(a, b, preferred_element_type=F32)


def grads_of(gate, up, flow, out):
    size = gate.shape[1]
    gate_value = gate.astype(F32)
    logistic = jax.nn.sigmoid(gate_value)
    weighted = flow.astype(F32) * logistic
    out[:, size:] = (weighted * gate_value).astype(BF16)
    out[:, :size] = (
        weighted * up.astype(F32) * (1.0 + gate_value * (1.0 - logistic))
    ).astype(BF16)


def grads_kernel(bounds, cut, gate_any, up_any, flow_any, *refs):
    outs = refs[: len(bounds) + 1]
    gate, up, flow, sems = refs[len(bounds) + 1 :]
    copies = []
    for k, (lo, hi) in enumerate(bounds):
        columns = pl.ds(lo, hi - lo)
        copies.append(
            [
                pltpu.make_async_copy(source.at[:, columns], target.at[:, columns], sems.at[k, i])
                for i, (source, target) in enumerate(
                    ((gate_any, gate), (up_any, up), (flow_any, flow))
                )
            ]
        )
        for copy in copies[k]:
            copy.start()
    for k, (lo, hi) in enumerate(bounds):
        for copy in copies[k]:
            copy.wait()
        whole = slice(0, gate.shape[0])
        parts = [(outs[k], whole)]
        if k == len(bounds) - 1:
            parts = [(outs[k], slice(0, cut)), (outs[k + 1], slice(cut, gate.shape[0]))]
        for out, rows in parts:
            grads_of(gate[rows, lo:hi], up[rows, lo:hi], flow[rows, lo:hi], out)


def join_kernel(a, b, out):
    n = a.shape[0]
    out[:n] = a[...]
    out[n:] = b[...]


def near_block(near, ident):
    row = lax.axis_index("row")
    k = wrap(ident - row, 4)
    return near[k, lax.rem(ident // 4 + row // 4, 2)]


def lend_tokens_kernel(own, above, far, below, out, near):
    col, sign = place()
    for i, ref in enumerate((own, above, far, below)):
        near[i] = ref[...]
    for i in range(3):
        out[i] = near_block(near, wrap(col - sign * (7 - i)))


def tokens_kernel(cut, near, got, out, laid):
    col, sign = place()
    rows, width = near.shape[2:]
    slab = width // 4
    rest = rows - cut

    def put(at, value):
        laid[at * cut : (at + 1) * cut] = value[:cut]
        laid[8 * cut + at * rest : 8 * cut + (at + 1) * rest] = value[cut:]

    for s, at in enumerate(MINE):
        put(at, near_block(near, wrap(col - sign * s)))
    for i, at in enumerate(LENT):
        put(at, got[i])
    for i, flip in enumerate((0, 2, 1, 3)):
        q = lax.axis_index("dp") ^ flip
        columns = pl.ds(pl.multiple_of(q * slab, slab), slab)
        for t in range(0, 8 * rows, TILE):
            out[i * slab : (i + 1) * slab, t : t + TILE] = laid[t : t + TILE, columns].T


def lay(pieces, cut, out, base, column, size):
    own, first, second, third, last = pieces
    n = own.shape[0]
    rest = n - cut
    blocks = [(own, 0), (first, 0), (first, n), (second, 0), (second, n), (third, 0), (third, n), (last, 0)]
    for at, (ref, start) in enumerate(blocks):
        out[base + at * cut : base + (at + 1) * cut, column : column + size] = ref[start : start + cut]
        if rest:
            begin = base + 8 * cut + at * rest
            out[begin : begin + rest, column : column + size] = ref[start + cut : start + n]


def weight_tiles(xt, cat, send, keep):
    half = xt.shape[0] // 2

    @pl.loop(0, cat.shape[1] // TILE)
    def _(t):
        columns = pl.ds(pl.multiple_of(t * TILE, TILE), TILE)
        grads = cat[:, columns]
        send[:, columns] = jnp.dot(xt[half:], grads, preferred_element_type=F32).astype(BF16)
        keep[:, columns] = jnp.dot(xt[:half], grads, preferred_element_type=F32)


def weight_kernel(cut, own, first, second, third, last, xt, cat, send, keep):
    lay((own, first, second, third, last), cut, cat, 0, 0, own.shape[1])
    weight_tiles(xt, cat, send, keep)


def weight_tail_kernel(*refs):
    early, late = refs[:5], refs[5:10]
    xt, send, keep, cat = refs[10:]
    n = early[0].shape[0]
    lay(early, n, cat, 0, 0, cat.shape[1])
    lay(late, late[0].shape[0], cat, 8 * n, 0, cat.shape[1])
    weight_tiles(xt, cat, send, keep)


def pair_kernel(keep, got, near, far):
    slab = keep.shape[0] // 2
    near[...] = keep[:slab] + got[:slab].astype(F32)
    far[...] = (keep[slab:] + got[slab:].astype(F32)).astype(BF16)


def score_kernel(lo, aliased, near, far, w_gate, w_up, *refs):
    out_gate, out_up, slab_gate, slab_up, res_gate, res_up, sems = refs[2 if aliased else 0 :]
    replica = lax.axis_index("dp")
    slab, size = slab_gate.shape
    rows = pl.ds(pl.multiple_of(replica * slab, slab), slab)
    read = [
        pltpu.make_async_copy(w.at[rows, pl.ds(lo, size)], target, sems.at[i])
        for i, (w, target) in enumerate(((w_gate, slab_gate), (w_up, slab_up)))
    ]
    write = [
        pltpu.make_async_copy(value, out.at[:, pl.ds(lo, size)], sems.at[2 + i])
        for i, (value, out) in enumerate(((res_gate, out_gate), (res_up, out_up)))
    ]
    for copy in read:
        copy.start()
    for i, (w, value) in enumerate(((slab_gate, res_gate), (slab_up, res_up))):
        read[i].wait()
        columns = slice(i * size, (i + 1) * size)
        value[...] = -w[...].astype(F32) * (near[:, columns] + far[:, columns].astype(F32))
        write[i].start()
    for copy in write:
        copy.wait()


def turn_kernel(lo, w_gate, w_up, out, held, sems):
    size = out.shape[0] // 2
    copies = [
        pltpu.make_async_copy(w.at[:, pl.ds(lo, size)], held.at[i], sems.at[i])
        for i, w in enumerate((w_gate, w_up))
    ]
    for copy in copies:
        copy.start()
    for i, copy in enumerate(copies):
        copy.wait()
        for t in range(0, size, 128):
            out[i * size + t : i * size + t + 128, :] = held[i, :, t : t + 128].T


def tokens_part_kernel(cat, turned, *refs):
    first, out = refs if len(refs) == 2 else (None, refs[0])

    @pl.loop(0, out.shape[1] // TILE)
    def _(t):
        columns = pl.ds(pl.multiple_of(t * TILE, TILE), TILE)
        total = mm(cat[...], turned[:, columns])
        out[:, columns] = total if first is None else total + first[:, columns]


def tokens_last_kernel(at, own, first, second, third, last, part, turned, mine, lend, cat):
    r = own.shape[0]
    lay((own, first, second, third, last), r, cat, 0, 0, own.shape[1])
    for t in range(0, turned.shape[1], TILE):
        columns = slice(t, t + TILE)
        total = mm(cat[...], turned[:, columns]) + part[at : at + 8 * r, columns]
        for out, places in ((mine, MINE), (lend, LENT)):
            for i, p in enumerate(places):
                out[i * r : (i + 1) * r, columns] = total[p * r : (p + 1) * r].astype(BF16)


def spread_kernel(mine, back, up, far, down, hold, every):
    col, sign = place()
    row = lax.axis_index("row")
    r = every.shape[2]
    blocks = [(s, mine, s) for s in range(5)] + [(7 - i, back, i) for i in range(3)]
    for s, ref, i in blocks:
        ident = wrap(col - sign * s)
        every[wrap(ident - row, 4), lax.rem(ident // 4 + row // 4, 2)] = ref[i * r : (i + 1) * r]
    for i, out in enumerate((hold, up, far, down)):
        out[...] = every[i]


def sum_y_kernel(hold, a, b, c, own, send):
    def total(j):
        return (hold[j].astype(F32) + a[j].astype(F32)) + (b[j].astype(F32) + c[j].astype(F32))

    own[...] = total(0)
    send[...] = total(1).astype(BF16)


def last_kernel(own_early, got_early, own_late, got_late, out):
    cut = own_early.shape[0]
    out[:cut] = (own_early[...] + got_early[...].astype(F32)).astype(BF16)
    out[cut:] = (own_late[...] + got_late[...].astype(F32)).astype(BF16)


def relay_kernel(*refs):
    pass


def shards(tokens, gate_pre, up_pre, d_hidden, w_gate, w_up):
    rows, width = tokens.shape
    hidden = gate_pre.shape[1]
    slab = width // 4
    cut = FIRST_ROWS
    rest = rows - cut
    many = 8 * rows
    mib = 1 << 20
    bounds, at = [], 0
    for parts in GROUPS:
        size = hidden * parts // sum(GROUPS)
        bounds.append((at, at + size))
        at += size

    run = Order()
    some = jax.ShapeDtypeStruct

    def fixed(*arrays):
        return [(pltpu.with_memory_space_constraint(a, pltpu.HBM), ANY) for a in arrays]

    weights = fixed(w_gate, w_up)

    def v(*arrays):
        return [(a, VMEM) for a in arrays]

    def one(kernel, shape, dtype, arrays, limit, scratch=()):
        return run(kernel, [(some, shape, dtype, VMEM)], v(*arrays), scratch, limit * mib)[0]

    def join(a, b):
        return one(join_kernel, (2 * a.shape[0],) + a.shape[1:], BF16, (a, b), 3)

    def relay(*values):
        return run(
            relay_kernel,
            [(some, value.shape, value.dtype, ANY) for value in values],
            [(value, ANY) for value in values],
            limit=mib,
            alias={i: i for i in range(len(values))},
        )

    def turn(bound):
        size = bound[1] - bound[0]
        return run(
            functools.partial(turn_kernel, bound[0]),
            [(some, (2 * size, width), BF16, VMEM)],
            weights,
            [pltpu.VMEM((2, width, size), BF16), pltpu.SemaphoreType.DMA((2,))],
            9 * mib,
            work=3,
        )[0]

    def weight_outs(cols):
        return [(some, (2 * slab, cols), BF16, VMEM), (some, (2 * slab, cols), F32, VMEM)]

    def weight_grads(pieces):
        cols = pieces[0].shape[1]
        outs = [(some, (many, cols), BF16, VMEM)] + weight_outs(cols)
        return run(functools.partial(weight_kernel, cut), outs, v(*pieces, xt), limit=19 * mib, work=4)

    def pair_sum(keep, got):
        cols = keep.shape[1]
        outs = [(some, (slab, cols), F32, VMEM), (some, (slab, cols), BF16, VMEM)]
        near, far = run(pair_kernel, outs, v(keep, got), limit=9 * mib, work=0.5)
        return near, swap_chip(far)

    def scores(near, far, bound, before):
        lo, hi = bound
        size = hi - lo
        scratch = (
            [pltpu.VMEM((slab, size), BF16)] * 2
            + [pltpu.VMEM((slab, size), F32)] * 2
            + [pltpu.SemaphoreType.DMA((4,))]
        )
        return run(
            functools.partial(score_kernel, lo, bool(before)),
            [(pltpu.HBM, (slab, hidden), F32, ANY)] * 2,
            v(near, far) + weights + fixed(*before),
            scratch,
            8 * mib,
            {4: 0, 5: 1} if before else None,
            2,
        )

    def tokens_last(pieces, part, at, turned):
        r, cols = pieces[0].shape
        mine, lend = run(
            functools.partial(tokens_last_kernel, at),
            [(some, (5 * r, width), BF16, VMEM), (some, (3 * r, width), BF16, VMEM)],
            v(*pieces, part, turned),
            [pltpu.VMEM((8 * r, cols), BF16)],
            16 * mib,
            work=4,
        )
        return mine, swap_core(lend)

    def tokens_part(cat, turned, *before):
        return run(
            tokens_part_kernel,
            [(some, (many, width), F32, VMEM)],
            v(cat, turned, *before),
            limit=18 * mib,
            work=4,
        )[0]

    def spread(mine, back, r):
        up, far, down, hold = run(
            spread_kernel,
            [(some, (2, r, width), BF16, VMEM)] * 4,
            v(mine, back),
            [pltpu.VMEM((4, 2, r, width), BF16)],
            limit=6 * mib,
        )
        return hold, along_y(up, 1), along_y(far, 2), along_y(down, -1)

    def sum_y(parts):
        r = parts[0].shape[1]
        outs = [(some, (r, width), F32, VMEM), (some, (r, width), BF16, VMEM)]
        own, send = run(sum_y_kernel, outs, v(*parts), limit=4 * mib)
        return own, swap_pair(send)

    sizes = [2 * (hi - lo) for lo, hi in bounds]
    shapes = [(n, size) for n, size in zip((rows, rows, cut, rest), sizes + sizes[-1:])]
    g0, g1, g2, g3 = run(
        functools.partial(grads_kernel, bounds, cut),
        [(some, shape, BF16, VMEM) for shape in shapes],
        fixed(gate_pre, up_pre, d_hidden),
        [pltpu.VMEM((rows, hidden), BF16)] * 3 + [pltpu.SemaphoreType.DMA((len(bounds), 3))],
        limit=5 * mib,
    )
    a1 = around(join(g0, swap_core(g0)))
    b1 = around(join(g1, swap_core(g1)))
    both = join(tokens[None], swap_pair(tokens)[None])
    near = (both, along_y(both, -1), along_y(both, 2), along_y(both, 1))
    c0 = join(g2, swap_core(g2))
    d0 = join(g3, swap_core(g3))
    turned0 = turn(bounds[0])
    a1 = relay(a1)[0]
    a2 = around(a1)
    b1 = relay(b1)[0]
    b2 = around(b1)
    turned1 = turn(bounds[1])
    a2, c0 = relay(a2, c0)
    a3, c1 = around(a2), around(c0)
    turned2 = turn(bounds[2])
    b2, d0 = relay(b2, d0)
    b3, d1 = around(b2), around(d0)
    lend, near = run(
        lend_tokens_kernel,
        [(some, (3, rows, width), BF16, VMEM), (some, (4, 2, rows, width), BF16, VMEM)],
        v(*near),
        limit=8 * mib,
    )
    lent = swap_core(lend)
    a3, c1 = relay(a3, c1)
    a4, c2 = around(a3[:rows]), around(c1)
    xt = one(
        functools.partial(tokens_kernel, cut),
        (width, many),
        BF16,
        (near, lent),
        11,
        [pltpu.VMEM((many, width), BF16)],
    )
    b3, d1 = relay(b3, d1)
    b4, d2 = around(b3[:rows]), around(d1)
    a4, c2 = relay(a4, c2)
    c3 = around(c2)
    cat0, send0, keep0 = weight_grads((g0, a1, a2, a3, a4))
    got0 = swap_core(send0)
    b4, d2 = relay(b4, d2)
    d3 = around(d2)
    near0, far0 = pair_sum(keep0, got0)
    cat1, send1, keep1 = weight_grads((g1, b1, b2, b3, b4))
    got1 = swap_core(send1)
    c3 = relay(c3)[0]
    c4 = around(c3[:cut])
    part = tokens_part(cat0, turned0)
    d3 = relay(d3)[0]
    d4 = around(d3[:rest])
    near1, far1 = pair_sum(keep1, got1)
    far0 = relay(far0)[0]
    part = tokens_part(cat1, turned1, part)
    early = (g2, c1, c2, c3, c4)
    tail = (g3, d1, d2, d3, d4)
    mine_early, back_early = tokens_last(early, part, 0, turned2)
    send2, keep2 = run(
        weight_tail_kernel,
        weight_outs(sizes[2]),
        v(*early, *tail, xt),
        [pltpu.VMEM((many, sizes[2]), BF16)],
        limit=15 * mib,
        work=4,
    )
    got2 = swap_core(send2)
    parts_early = spread(mine_early, back_early, cut)
    mine_late, back_late = tokens_last(tail, part, 8 * cut, turned2)
    near2, far2 = pair_sum(keep2, got2)
    far1 = relay(far1)[0]
    parts_late = spread(mine_late, back_late, rest)
    done = scores(near0, far0, bounds[0], ())
    own_early, got_early = sum_y(parts_early)
    done = scores(near1, far1, bounds[1], done)
    own_late, got_late = sum_y(parts_late)
    done = scores(near2, far2, bounds[2], done)
    d_tokens = one(
        last_kernel, (rows, width), BF16, (own_early, got_early, own_late, got_late), 4
    )
    score_gate, score_up = [d.reshape(1, 1, slab, hidden) for d in done]
    return (d_tokens, score_gate, score_up)


def solution(mesh):
    placed = (
        P(("dp", "row"), "col"),
        P(("dp", "col"), "row"),
        P(("dp", "col"), "row"),
        P(("dp", "col"), "row"),
        P("col", "row"),
        P("col", "row"),
    )
    return jax.shard_map(
        shards,
        mesh=mesh,
        in_specs=placed,
        out_specs=(
            P(("dp", "row"), "col"),
            P("col", "dp", None, "row"),
            P("col", "dp", None, "row"),
        ),
        check_vma=False,
    )
```

```python
import functools

import jax
import jax.numpy as jnp
from jax import lax
from jax.experimental import pallas as pl
from jax.experimental.pallas import tpu as pltpu
from jax.sharding import PartitionSpec as P

F32 = jnp.float32
BF16 = jnp.bfloat16
GROUPS = (5, 5, 4)
TILE = 256
SCALE = 1000000000
VMEM = pl.BlockSpec(memory_space=pltpu.VMEM)
ANY = pl.BlockSpec(memory_space=pl.ANY)
MINE = (0, 1, 3, 5, 7)
LENT = (2, 4, 6)


def around(value):
    perm = []
    for dp in range(4):
        step = 1 if dp % 2 == 0 else -1
        for z in range(8):
            perm.append((dp * 8 + z, dp * 8 + (z + step) % 8))
    return lax.ppermute(value, ("dp", "col"), perm)


def swap_core(value):
    return lax.ppermute(value, "dp", [(i, i ^ 1) for i in range(4)])


def swap_chip(value):
    return lax.ppermute(value, "dp", [(i, i ^ 2) for i in range(4)])


def swap_pair(value):
    return lax.ppermute(value, "row", [(i, i ^ 4) for i in range(8)])


def along_y(value, step):
    return lax.ppermute(
        value, "row", [(i, (i // 4) * 4 + (i % 4 + step) % 4) for i in range(8)]
    )


def place():
    col = lax.axis_index("col")
    sign = 1 - 2 * lax.rem(lax.axis_index("dp"), 2)
    return col, sign


def wrap(v, n=8):
    return lax.rem(v + 8 * n, n)


class Order:
    def __init__(self):
        self.before = ()

    def __call__(self, kernel, outs, ins, scratch=(), limit=None, alias=None, work=0.3):
        count, waits = len(ins), len(self.before)

        def body(*refs):
            kernel(*refs[:count], *refs[count + waits :])

        got = pl.pallas_call(
            body,
            out_shape=[make(shape, dtype) for make, shape, dtype, _ in outs],
            in_specs=[spec for _, spec in ins] + [ANY] * waits,
            out_specs=[spec for _, _, _, spec in outs],
            scratch_shapes=list(scratch),
            input_output_aliases=alias or {},
            compiler_params=pltpu.CompilerParams(vmem_limit_bytes=limit),
            cost_estimate=pl.CostEstimate(
                flops=int(work * SCALE), bytes_accessed=1, transcendentals=0
            ),
        )(*[a for a, _ in ins], *self.before)
        held = got[-1]
        if outs[-1][0] is pltpu.HBM:
            held = pltpu.with_memory_space_constraint(held, pltpu.HBM)
        self.before = (held,)
        return got


def mm(a, b):
    return jnp.dot(a, b, preferred_element_type=F32)


def grads_of(gate, up, flow, out):
    size = gate.shape[1]
    gate_value = gate.astype(F32)
    logistic = jax.nn.sigmoid(gate_value)
    weighted = flow.astype(F32) * logistic
    out[:, size:] = (weighted * gate_value).astype(BF16)
    out[:, :size] = (
        weighted * up.astype(F32) * (1.0 + gate_value * (1.0 - logistic))
    ).astype(BF16)


def grads_kernel(bounds, gate_any, up_any, flow_any, *refs):
    outs = refs[: len(bounds)]
    gate, up, flow, sems = refs[len(bounds) :]
    copies = []
    for k, (lo, hi) in enumerate(bounds):
        columns = pl.ds(lo, hi - lo)
        copies.append(
            [
                pltpu.make_async_copy(source.at[:, columns], target.at[:, columns], sems.at[k, i])
                for i, (source, target) in enumerate(
                    ((gate_any, gate), (up_any, up), (flow_any, flow))
                )
            ]
        )
        for copy in copies[k]:
            copy.start()
    for k, (lo, hi) in enumerate(bounds):
        for copy in copies[k]:
            copy.wait()
        grads_of(gate[:, lo:hi], up[:, lo:hi], flow[:, lo:hi], outs[k])


def join_kernel(a, b, out):
    n = a.shape[0]
    out[:n] = a[...]
    out[n:] = b[...]


def near_block(near, ident):
    row = lax.axis_index("row")
    k = wrap(ident - row, 4)
    return near[k, lax.rem(ident // 4 + row // 4, 2)]


def lend_tokens_kernel(own, above, far, below, out, near):
    col, sign = place()
    for i, ref in enumerate((own, above, far, below)):
        near[i] = ref[...]
    for i in range(3):
        out[i] = near_block(near, wrap(col - sign * (7 - i)))


def tokens_kernel(near, got, out, laid):
    col, sign = place()
    rows, width = near.shape[2:]
    slab = width // 4
    for s, at in enumerate(MINE):
        laid[at * rows : (at + 1) * rows] = near_block(near, wrap(col - sign * s))
    for i, at in enumerate(LENT):
        laid[at * rows : (at + 1) * rows] = got[i]
    for i, flip in enumerate((0, 2, 1, 3)):
        q = lax.axis_index("dp") ^ flip
        columns = pl.ds(pl.multiple_of(q * slab, slab), slab)
        for t in range(0, 8 * rows, TILE):
            out[i * slab : (i + 1) * slab, t : t + TILE] = laid[t : t + TILE, columns].T


def lay(pieces, cat):
    at = 0
    for piece in pieces:
        cat[at : at + piece.shape[0]] = piece[...]
        at += piece.shape[0]


def weight_kernel(own, first, second, third, last, xt, cat, *outs):
    lay((own, first, second, third, last), cat)
    slab = xt.shape[0] // 4

    @pl.loop(0, cat.shape[1] // TILE)
    def _(t):
        columns = pl.ds(pl.multiple_of(t * TILE, TILE), TILE)
        total = mm(xt[...], cat[:, columns])
        for i, out in enumerate(outs):
            out[:, columns] = total[i * slab : (i + 1) * slab].astype(out.dtype)


def pair_kernel(keep, got, far):
    far[...] = (keep[...] + got[...].astype(F32)).astype(BF16)


def score_kernel(lo, aliased, near, got, far, w_gate, w_up, *refs):
    out_gate, out_up, slab_gate, slab_up, res_gate, res_up, sems = refs[2 if aliased else 0 :]
    replica = lax.axis_index("dp")
    slab, size = slab_gate.shape
    rows = pl.ds(pl.multiple_of(replica * slab, slab), slab)
    read = [
        pltpu.make_async_copy(w.at[rows, pl.ds(lo, size)], target, sems.at[i])
        for i, (w, target) in enumerate(((w_gate, slab_gate), (w_up, slab_up)))
    ]
    write = [
        pltpu.make_async_copy(value, out.at[:, pl.ds(lo, size)], sems.at[2 + i])
        for i, (value, out) in enumerate(((res_gate, out_gate), (res_up, out_up)))
    ]
    for copy in read:
        copy.start()
    for i, (w, value) in enumerate(((slab_gate, res_gate), (slab_up, res_up))):
        read[i].wait()
        columns = slice(i * size, (i + 1) * size)
        total = near[:, columns] + got[:, columns].astype(F32) + far[:, columns].astype(F32)
        value[...] = -w[...].astype(F32) * total
        write[i].start()
    for copy in write:
        copy.wait()


def turn_kernel(lo, w_gate, w_up, out, held, sems):
    size = out.shape[0] // 2
    copies = [
        pltpu.make_async_copy(w.at[:, pl.ds(lo, size)], held.at[i], sems.at[i])
        for i, w in enumerate((w_gate, w_up))
    ]
    for copy in copies:
        copy.start()
    for i, copy in enumerate(copies):
        copy.wait()
        for t in range(0, size, 128):
            out[i * size + t : i * size + t + 128, :] = held[i, :, t : t + 128].T


def tokens_part_kernel(cat, turned, *refs):
    first, out = refs if len(refs) == 2 else (None, refs[0])

    @pl.loop(0, out.shape[1] // TILE)
    def _(t):
        columns = pl.ds(pl.multiple_of(t * TILE, TILE), TILE)
        total = mm(cat[...], turned[:, columns])
        out[:, columns] = total if first is None else total + first[:, columns]


def tokens_last_kernel(own, first, second, third, last, part, turned, mine, lend, cat):
    r = own.shape[0]
    lay((own, first, second, third, last), cat)
    for t in range(0, turned.shape[1], TILE):
        columns = slice(t, t + TILE)
        total = mm(cat[...], turned[:, columns]) + part[:, columns]
        for out, places in ((mine, MINE), (lend, LENT)):
            for i, p in enumerate(places):
                out[i * r : (i + 1) * r, columns] = total[p * r : (p + 1) * r].astype(BF16)


def spread_kernel(mine, back, *refs):
    outs, every = refs[:-1], refs[-1]
    col, sign = place()
    row = lax.axis_index("row")
    r = every.shape[2]
    blocks = [(s, mine, s) for s in range(5)] + [(7 - i, back, i) for i in range(3)]
    for s, ref, i in blocks:
        ident = wrap(col - sign * s)
        every[wrap(ident - row, 4), lax.rem(ident // 4 + row // 4, 2)] = ref[i * r : (i + 1) * r]
    for i, out in enumerate(outs):
        out[...] = every[i]


def sum_y_kernel(hold, a, b, c, own, send):
    def total(j):
        return (hold[j].astype(F32) + a[j].astype(F32)) + (b[j].astype(F32) + c[j].astype(F32))

    own[...] = total(0)
    send[...] = total(1).astype(BF16)


def last_kernel(own, got, out):
    out[...] = (own[...] + got[...].astype(F32)).astype(BF16)


def relay_kernel(*refs):
    pass


def shards(tokens, gate_pre, up_pre, d_hidden, w_gate, w_up):
    rows, width = tokens.shape
    hidden = gate_pre.shape[1]
    slab = width // 4
    many = 8 * rows
    mib = 1 << 20
    bounds, at = [], 0
    for parts in GROUPS:
        size = hidden * parts // sum(GROUPS)
        bounds.append((at, at + size))
        at += size

    run = Order()
    some = jax.ShapeDtypeStruct

    def fixed(*arrays):
        return [(pltpu.with_memory_space_constraint(a, pltpu.HBM), ANY) for a in arrays]

    weights = fixed(w_gate, w_up)

    def v(*arrays):
        return [(a, VMEM) for a in arrays]

    def one(kernel, shape, dtype, arrays, limit, scratch=()):
        return run(kernel, [(some, shape, dtype, VMEM)], v(*arrays), scratch, limit * mib)[0]

    def join(a, b):
        return one(join_kernel, (2 * a.shape[0],) + a.shape[1:], BF16, (a, b), 3)

    def relay(*values):
        return run(
            relay_kernel,
            [(some, value.shape, value.dtype, ANY) for value in values],
            [(value, ANY) for value in values],
            limit=mib,
            alias={i: i for i in range(len(values))},
        )

    def turn(bound):
        size = bound[1] - bound[0]
        return run(
            functools.partial(turn_kernel, bound[0]),
            [(some, (2 * size, width), BF16, VMEM)],
            weights,
            [pltpu.VMEM((2, width, size), BF16), pltpu.SemaphoreType.DMA((2,))],
            9 * mib,
            work=3,
        )[0]

    def weight_grads(pieces):
        cols = pieces[0].shape[1]
        outs = [(some, (many, cols), BF16, VMEM)]
        outs += [(some, (slab, cols), dtype, VMEM) for dtype in (F32, F32, BF16, BF16)]
        cat, near, far, send_near, send_far = run(
            weight_kernel, outs, v(*pieces, xt), limit=19 * mib, work=4
        )
        return cat, (near, swap_core(send_near)), (far, swap_core(send_far))

    def pair_sum(parts):
        return swap_chip(one(pair_kernel, parts[0].shape, BF16, parts, 6))

    def scores(near, far, bound, before):
        near, got = near
        lo, hi = bound
        size = hi - lo
        scratch = (
            [pltpu.VMEM((slab, size), BF16)] * 2
            + [pltpu.VMEM((slab, size), F32)] * 2
            + [pltpu.SemaphoreType.DMA((4,))]
        )
        return run(
            functools.partial(score_kernel, lo, bool(before)),
            [(pltpu.HBM, (slab, hidden), F32, ANY)] * 2,
            v(near, got, far) + weights + fixed(*before),
            scratch,
            8 * mib,
            {5: 0, 6: 1} if before else None,
            2,
        )

    def tokens_last(pieces, part, turned):
        cols = pieces[0].shape[1]
        mine, lend = run(
            tokens_last_kernel,
            [(some, (5 * rows, width), BF16, VMEM), (some, (3 * rows, width), BF16, VMEM)],
            v(*pieces, part, turned),
            [pltpu.VMEM((many, cols), BF16)],
            17 * mib,
            work=4,
        )
        return mine, swap_core(lend)

    def tokens_part(cat, turned, *before):
        return run(
            tokens_part_kernel,
            [(some, (many, width), F32, VMEM)],
            v(cat, turned, *before),
            limit=18 * mib,
            work=4,
        )[0]

    def spread(mine, back):
        hold, up, far, down = run(
            spread_kernel,
            [(some, (2, rows, width), BF16, VMEM)] * 4,
            v(mine, back),
            [pltpu.VMEM((4, 2, rows, width), BF16)],
            limit=8 * mib,
        )
        return hold, along_y(up, 1), along_y(far, 2), along_y(down, -1)

    def sum_y(parts):
        r = parts[0].shape[1]
        outs = [(some, (r, width), F32, VMEM), (some, (r, width), BF16, VMEM)]
        own, send = run(sum_y_kernel, outs, v(*parts), limit=4 * mib)
        return own, swap_pair(send)

    sizes = [2 * (hi - lo) for lo, hi in bounds]
    g0, g1, g2 = run(
        functools.partial(grads_kernel, bounds),
        [(some, (rows, size), BF16, VMEM) for size in sizes],
        fixed(gate_pre, up_pre, d_hidden),
        [pltpu.VMEM((rows, hidden), BF16)] * 3 + [pltpu.SemaphoreType.DMA((len(bounds), 3))],
        limit=5 * mib,
    )
    a1 = around(join(g0, swap_core(g0)))
    b1 = around(join(g1, swap_core(g1)))
    c0 = join(g2, swap_core(g2))
    turned0 = turn(bounds[0])
    a1, c0 = relay(a1, c0)
    a2, c1 = around(a1), around(c0)
    both = join(tokens[None], swap_pair(tokens)[None])
    above, below = along_y(both, -1), along_y(both, 1)
    b1 = relay(b1)[0]
    b2 = around(b1)
    turned1 = turn(bounds[1])
    a2 = relay(a2)[0]
    a3 = around(a2)
    c1 = relay(c1)[0]
    c2 = around(c1)
    b2, above, below = relay(b2, above, below)
    b3 = around(b2)
    far = along_y(both, 2)
    turned2 = turn(bounds[2])
    a3 = relay(a3)[0]
    a4 = around(a3[:rows])
    c2 = relay(c2)[0]
    c3 = around(c2)
    b3, far = relay(b3, far)
    b4 = around(b3[:rows])
    lend, near = run(
        lend_tokens_kernel,
        [(some, (3, rows, width), BF16, VMEM), (some, (4, 2, rows, width), BF16, VMEM)],
        v(both, above, far, below),
        limit=8 * mib,
    )
    lent = swap_core(lend)
    xt = one(
        tokens_kernel,
        (width, many),
        BF16,
        (near, lent),
        11,
        [pltpu.VMEM((many, width), BF16)],
    )
    cat0, near0, far0 = weight_grads((g0, a1, a2, a3, a4))
    part = tokens_part(cat0, turned0)
    c3, b4 = relay(c3, b4)
    c4 = around(c3[:rows])
    far0 = pair_sum(far0)
    cat1, near1, far1 = weight_grads((g1, b1, b2, b3, b4))
    part = tokens_part(cat1, turned1, part)
    c4 = relay(c4)[0]
    far0 = relay(far0)[0]
    far1 = pair_sum(far1)
    pieces = (g2, c1, c2, c3, c4)
    mine, back = tokens_last(pieces, part, turned2)
    _, near2, far2 = weight_grads(pieces)
    parts = spread(mine, back)
    far2 = pair_sum(far2)
    done = scores(near0, far0, bounds[0], ())
    done = scores(near1, far1, bounds[1], done)
    own, got = sum_y(parts)
    done = scores(near2, far2, bounds[2], done)
    d_tokens = one(last_kernel, (rows, width), BF16, (own, got), 4)
    score_gate, score_up = [d.reshape(1, 1, slab, hidden) for d in done]
    return (d_tokens, score_gate, score_up)


def solution(mesh):
    placed = (
        P(("dp", "row"), "col"),
        P(("dp", "col"), "row"),
        P(("dp", "col"), "row"),
        P(("dp", "col"), "row"),
        P("col", "row"),
        P("col", "row"),
    )
    return jax.shard_map(
        shards,
        mesh=mesh,
        in_specs=placed,
        out_specs=(
            P(("dp", "row"), "col"),
            P("col", "dp", None, "row"),
            P("col", "dp", None, "row"),
        ),
        check_vma=False,
    )
```

```python
import functools

import jax
import jax.numpy as jnp
from jax import lax
from jax.experimental import pallas as pl
from jax.experimental.pallas import tpu as pltpu
from jax.sharding import PartitionSpec as P

F32 = jnp.float32
BF16 = jnp.bfloat16
GROUPS = (5, 5, 4)
TILE = 256
SCALE = 1000000000
VMEM = pl.BlockSpec(memory_space=pltpu.VMEM)
ANY = pl.BlockSpec(memory_space=pl.ANY)
MINE = (0, 1, 3, 5, 7)
LENT = (2, 4, 6)


def around(value):
    perm = []
    for dp in range(4):
        step = 1 if dp % 2 == 0 else -1
        for z in range(8):
            perm.append((dp * 8 + z, dp * 8 + (z + step) % 8))
    return lax.ppermute(value, ("dp", "col"), perm)


def swap_core(value):
    return lax.ppermute(value, "dp", [(i, i ^ 1) for i in range(4)])


def swap_chip(value):
    return lax.ppermute(value, "dp", [(i, i ^ 2) for i in range(4)])


def swap_pair(value):
    return lax.ppermute(value, "row", [(i, i ^ 4) for i in range(8)])


def along_y(value, step):
    return lax.ppermute(
        value, "row", [(i, (i // 4) * 4 + (i % 4 + step) % 4) for i in range(8)]
    )


def place():
    col = lax.axis_index("col")
    sign = 1 - 2 * lax.rem(lax.axis_index("dp"), 2)
    return col, sign


def wrap(v, n=8):
    return lax.rem(v + 8 * n, n)


class Order:
    def __init__(self):
        self.before = ()

    def __call__(self, kernel, outs, ins, scratch=(), limit=None, alias=None, work=0.3):
        count, waits = len(ins), len(self.before)

        def body(*refs):
            kernel(*refs[:count], *refs[count + waits :])

        got = pl.pallas_call(
            body,
            out_shape=[make(shape, dtype) for make, shape, dtype, _ in outs],
            in_specs=[spec for _, spec in ins] + [ANY] * waits,
            out_specs=[spec for _, _, _, spec in outs],
            scratch_shapes=list(scratch),
            input_output_aliases=alias or {},
            compiler_params=pltpu.CompilerParams(vmem_limit_bytes=limit),
            cost_estimate=pl.CostEstimate(
                flops=int(work * SCALE), bytes_accessed=1, transcendentals=0
            ),
        )(*[a for a, _ in ins], *self.before)
        self.before = (got[-1],)
        return got


def mm(a, b):
    return jnp.dot(a, b, preferred_element_type=F32)


def grads_of(gate, up, flow, out):
    size = gate.shape[1]
    gate_value = gate.astype(F32)
    logistic = jax.nn.sigmoid(gate_value)
    weighted = flow.astype(F32) * logistic
    out[:, size:] = (weighted * gate_value).astype(BF16)
    out[:, :size] = (
        weighted * up.astype(F32) * (1.0 + gate_value * (1.0 - logistic))
    ).astype(BF16)


def grads_kernel(bounds, gate_any, up_any, flow_any, *refs):
    outs = refs[: len(bounds)]
    gate, up, flow, sems = refs[len(bounds) :]
    copies = []
    for k, (lo, hi) in enumerate(bounds):
        columns = pl.ds(lo, hi - lo)
        copies.append(
            [
                pltpu.make_async_copy(source.at[:, columns], target.at[:, columns], sems.at[k, i])
                for i, (source, target) in enumerate(
                    ((gate_any, gate), (up_any, up), (flow_any, flow))
                )
            ]
        )
        for copy in copies[k]:
            copy.start()
    for k, (lo, hi) in enumerate(bounds):
        for copy in copies[k]:
            copy.wait()
        grads_of(gate[:, lo:hi], up[:, lo:hi], flow[:, lo:hi], outs[k])


def join_kernel(a, b, out):
    n = a.shape[0]
    out[:n] = a[...]
    out[n:] = b[...]


def near_block(near, ident):
    row = lax.axis_index("row")
    k = wrap(ident - row, 4)
    return near[k, lax.rem(ident // 4 + row // 4, 2)]


def lend_tokens_kernel(own, above, far, below, out0, out1, out2, near):
    col, sign = place()
    for i, ref in enumerate((own, above, far, below)):
        near[i] = ref[...]
    for i, out in enumerate((out0, out1, out2)):
        out[...] = near_block(near, wrap(col - sign * (7 - i)))


def tokens_kernel(near, got0, got1, got2, out, laid):
    col, sign = place()
    rows, width = near.shape[2:]
    slab = width // 4
    for s, at in enumerate(MINE):
        laid[at * rows : (at + 1) * rows] = near_block(near, wrap(col - sign * s))
    for got, at in zip((got0, got1, got2), LENT):
        laid[at * rows : (at + 1) * rows] = got[...]
    for i, flip in enumerate((0, 2, 1, 3)):
        q = lax.axis_index("dp") ^ flip
        columns = pl.ds(pl.multiple_of(q * slab, slab), slab)
        for t in range(0, 8 * rows, TILE):
            out[i * slab : (i + 1) * slab, t : t + TILE] = laid[t : t + TILE, columns].T


def lay(pieces, cat):
    at = 0
    for piece in pieces:
        cat[at : at + piece.shape[0]] = piece[...]
        at += piece.shape[0]


def weight_kernel(own, first, second, third, last, xt, cat, *outs):
    lay((own, first, second, third, last), cat)
    @pl.loop(0, cat.shape[1] // TILE)
    def _(t):
        columns = pl.ds(pl.multiple_of(t * TILE, TILE), TILE)
        total = mm(xt[...], cat[:, columns])
        at = 0
        for out in outs:
            n = out.shape[0]
            out[:, columns] = total[at : at + n].astype(out.dtype)
            at += n


def pair_kernel(keep, got0, got1, far):
    half = got0.shape[0]
    far[:half] = (keep[:half] + got0[...].astype(F32)).astype(BF16)
    far[half:] = (keep[half:] + got1[...].astype(F32)).astype(BF16)


def score_kernel(lo, aliased, near, got, far, w_gate, w_up, *refs):
    out_gate, out_up, mark, slab_gate, slab_up, res_gate, res_up, sems = refs[2 if aliased else 0 :]
    mark[...] = jnp.zeros_like(mark)
    replica = lax.axis_index("dp")
    slab, size = slab_gate.shape
    rows = pl.ds(pl.multiple_of(replica * slab, slab), slab)
    read = [
        pltpu.make_async_copy(w.at[rows, pl.ds(lo, size)], target, sems.at[i])
        for i, (w, target) in enumerate(((w_gate, slab_gate), (w_up, slab_up)))
    ]
    write = [
        pltpu.make_async_copy(value, out.at[:, pl.ds(lo, size)], sems.at[2 + i])
        for i, (value, out) in enumerate(((res_gate, out_gate), (res_up, out_up)))
    ]
    for copy in read:
        copy.start()
    for i, (w, value) in enumerate(((slab_gate, res_gate), (slab_up, res_up))):
        read[i].wait()
        columns = slice(i * size, (i + 1) * size)
        total = near[:, columns] + got[:, columns].astype(F32) + far[:, columns].astype(F32)
        value[...] = -w[...].astype(F32) * total
        write[i].start()
    for copy in write:
        copy.wait()


def turn_kernel(lo, w_gate, w_up, out, held, sems):
    size = out.shape[0] // 2
    copies = [
        pltpu.make_async_copy(w.at[:, pl.ds(lo, size)], held.at[i], sems.at[i])
        for i, w in enumerate((w_gate, w_up))
    ]
    for copy in copies:
        copy.start()
    for i, copy in enumerate(copies):
        copy.wait()
        for t in range(0, size, 128):
            out[i * size + t : i * size + t + 128, :] = held[i, :, t : t + 128].T


def tokens_part_kernel(cat, turned, out):
    @pl.loop(0, out.shape[1] // TILE)
    def _(t):
        columns = pl.ds(pl.multiple_of(t * TILE, TILE), TILE)
        out[:, columns] = mm(cat[...], turned[:, columns])


def tokens_last_kernel(*refs):
    unit1, unit2 = refs[:5], refs[5:10]
    part, turned1, turned2, mine, lend0, lend1, lend2, cat1, cat2 = refs[10:]
    r = unit1[0].shape[0]
    lay(unit1, cat1)
    lay(unit2, cat2)
    for t in range(0, turned1.shape[1], TILE):
        columns = slice(t, t + TILE)
        total = mm(cat1[...], turned1[:, columns]) + part[:, columns]
        total = total + mm(cat2[...], turned2[:, columns])
        for i, p in enumerate(MINE):
            mine[i * r : (i + 1) * r, columns] = total[p * r : (p + 1) * r].astype(BF16)
        for out, p in zip((lend0, lend1, lend2), LENT):
            out[:, columns] = total[p * r : (p + 1) * r].astype(BF16)


def spread_kernel(mine, back0, back1, back2, *refs):
    outs, every = refs[:-1], refs[-1]
    col, sign = place()
    row = lax.axis_index("row")
    r = every.shape[2]
    blocks = [(s, mine, s) for s in range(5)] + [(7, back0, 0), (6, back1, 0), (5, back2, 0)]
    for s, ref, i in blocks:
        ident = wrap(col - sign * s)
        every[wrap(ident - row, 4), lax.rem(ident // 4 + row // 4, 2)] = ref[i * r : (i + 1) * r]
    for i, out in enumerate(outs):
        out[...] = every[i]


def sum_y_kernel(hold, a, b, c, own, send):
    def total(j):
        return (hold[j].astype(F32) + a[j].astype(F32)) + (b[j].astype(F32) + c[j].astype(F32))

    own[...] = total(0)
    send[...] = total(1).astype(BF16)


def last_kernel(own, got, out, mark):
    mark[...] = jnp.zeros_like(mark)
    out[...] = (own[...] + got[...].astype(F32)).astype(BF16)


def relay_kernel(*refs):
    pass


def shards(tokens, gate_pre, up_pre, d_hidden, w_gate, w_up):
    rows, width = tokens.shape
    hidden = gate_pre.shape[1]
    slab = width // 4
    many = 8 * rows
    mib = 1 << 20
    bounds, at = [], 0
    for parts in GROUPS:
        size = hidden * parts // sum(GROUPS)
        bounds.append((at, at + size))
        at += size

    run = Order()
    some = jax.ShapeDtypeStruct

    def fixed(*arrays):
        return [(pltpu.with_memory_space_constraint(a, pltpu.HBM), ANY) for a in arrays]

    weights = fixed(w_gate, w_up)

    def v(*arrays):
        return [(a, VMEM) for a in arrays]

    def one(kernel, shape, dtype, arrays, limit, scratch=()):
        return run(kernel, [(some, shape, dtype, VMEM)], v(*arrays), scratch, limit * mib)[0]

    def join(a, b):
        return one(join_kernel, (2 * a.shape[0],) + a.shape[1:], BF16, (a, b), 3)

    def relay(*values):
        return run(
            relay_kernel,
            [(some, value.shape, value.dtype, ANY) for value in values],
            [(value, ANY) for value in values],
            limit=mib,
            alias={i: i for i in range(len(values))},
        )

    def turn(bound):
        size = bound[1] - bound[0]
        return run(
            functools.partial(turn_kernel, bound[0]),
            [(some, (2 * size, width), BF16, VMEM)],
            weights,
            [pltpu.VMEM((2, width, size), BF16), pltpu.SemaphoreType.DMA((2,))],
            9 * mib,
            work=3,
        )[0]

    def weight_grads(pieces):
        cols = pieces[0].shape[1]
        outs = [(some, (many, cols), BF16, VMEM)]
        outs += [(some, (slab, cols), dtype, VMEM) for dtype in (F32, F32, BF16)]
        outs += [(some, (slab // 2, cols), BF16, VMEM)] * 2
        cat, near, far, send_near, *send_far = run(
            weight_kernel, outs, v(*pieces, xt), limit=19 * mib, work=0.5
        )
        return cat, (near, swap_core(send_near)), (far, *[swap_core(part) for part in send_far])

    def pair_sum(parts):
        return swap_chip(one(pair_kernel, parts[0].shape, BF16, parts, 6))

    def scores(near, far, bound, before):
        near, got = near
        lo, hi = bound
        size = hi - lo
        scratch = (
            [pltpu.VMEM((slab, size), BF16)] * 2
            + [pltpu.VMEM((slab, size), F32)] * 2
            + [pltpu.SemaphoreType.DMA((4,))]
        )
        return run(
            functools.partial(score_kernel, lo, bool(before)),
            [(pltpu.HBM, (slab, hidden), F32, ANY)] * 2 + [(some, (8, 128), F32, VMEM)],
            v(near, got, far) + weights + fixed(*before),
            scratch,
            8 * mib,
            {5: 0, 6: 1} if before else None,
        )[:2]

    def tokens_last(unit1, unit2, part):
        outs = [(some, (5 * rows, width), BF16, VMEM)] + [(some, (rows, width), BF16, VMEM)] * 3
        mine, *lend = run(
            tokens_last_kernel,
            outs,
            v(*unit1, *unit2, part, turned1, turned2),
            [pltpu.VMEM((many, unit[0].shape[1]), BF16) for unit in (unit1, unit2)],
            27 * mib,
            work=1,
        )
        return mine, [swap_core(block) for block in lend]

    def tokens_part(cat, turned):
        return one(tokens_part_kernel, (many, width), F32, (cat, turned), 18)

    def spread(mine, back):
        hold, up, far, down = run(
            spread_kernel,
            [(some, (2, rows, width), BF16, VMEM)] * 4,
            v(mine, *back),
            [pltpu.VMEM((4, 2, rows, width), BF16)],
            limit=8 * mib,
        )
        return hold, along_y(up, 1), along_y(far, 2), along_y(down, -1)

    def sum_y(parts):
        r = parts[0].shape[1]
        outs = [(some, (r, width), F32, VMEM), (some, (r, width), BF16, VMEM)]
        own, send = run(sum_y_kernel, outs, v(*parts), limit=4 * mib)
        return own, swap_pair(send)

    sizes = [2 * (hi - lo) for lo, hi in bounds]
    g0, g1, g2 = run(
        functools.partial(grads_kernel, bounds),
        [(some, (rows, size), BF16, VMEM) for size in sizes],
        fixed(gate_pre, up_pre, d_hidden),
        [pltpu.VMEM((rows, hidden), BF16)] * 3 + [pltpu.SemaphoreType.DMA((len(bounds), 3))],
        limit=5 * mib,
    )
    a1 = around(join(g0, swap_core(g0)))
    b1 = around(join(g1, swap_core(g1)))
    c0 = join(g2, swap_core(g2))
    turned0 = turn(bounds[0])
    a1, c0 = relay(a1, c0)
    a2, c1 = around(a1), around(c0)
    both = join(tokens[None], swap_pair(tokens)[None])
    above, below = along_y(both, -1), along_y(both, 1)
    b1 = relay(b1)[0]
    b2 = around(b1)
    turned1 = turn(bounds[1])
    a2 = relay(a2)[0]
    a3 = around(a2)
    c1 = relay(c1)[0]
    c2 = around(c1)
    b2, above, below = relay(b2, above, below)
    b3 = around(b2)
    far = along_y(both, 2)
    turned2 = turn(bounds[2])
    a3 = relay(a3)[0]
    a4 = around(a3[:rows])
    c2 = relay(c2)[0]
    c3 = around(c2)
    b3, far = relay(b3, far)
    b4 = around(b3[:rows])
    *lend, near = run(
        lend_tokens_kernel,
        [(some, (rows, width), BF16, VMEM)] * 3 + [(some, (4, 2, rows, width), BF16, VMEM)],
        v(both, above, far, below),
        limit=8 * mib,
    )
    lent = [swap_core(block) for block in lend]
    a4 = relay(a4)[0]
    xt = one(
        tokens_kernel,
        (width, many),
        BF16,
        (near, *lent),
        11,
        [pltpu.VMEM((many, width), BF16)],
    )
    cat0, near0, far0 = weight_grads((g0, a1, a2, a3, a4))
    c3 = relay(c3)[0]
    c4 = around(c3[:rows])
    far0 = pair_sum(far0)
    part = tokens_part(cat0, turned0)
    b4 = relay(b4)[0]
    c4 = relay(c4)[0]
    unit1, unit2 = (g1, b1, b2, b3, b4), (g2, c1, c2, c3, c4)
    _, near1, far1 = weight_grads(unit1)
    mine, back = tokens_last(unit1, unit2, part)
    far1 = pair_sum(far1)
    far0 = relay(far0)[0]
    _, near2, far2 = weight_grads(unit2)
    parts = spread(mine, back)
    far2 = pair_sum(far2)
    done = scores(near0, far0, bounds[0], ())
    done = scores(near1, far1, bounds[1], done)
    own, got = sum_y(parts)
    outs = [(some, (rows, width), BF16, VMEM), (some, (8, 128), F32, VMEM)]
    d_tokens = run(last_kernel, outs, v(own, got), limit=4 * mib)[0]
    done = scores(near2, far2, bounds[2], done)
    score_gate, score_up = [d.reshape(1, 1, slab, hidden) for d in done]
    return (d_tokens, score_gate, score_up)


def solution(mesh):
    placed = (
        P(("dp", "row"), "col"),
        P(("dp", "col"), "row"),
        P(("dp", "col"), "row"),
        P(("dp", "col"), "row"),
        P("col", "row"),
        P("col", "row"),
    )
    return jax.shard_map(
        shards,
        mesh=mesh,
        in_specs=placed,
        out_specs=(
            P(("dp", "row"), "col"),
            P("col", "dp", None, "row"),
            P("col", "dp", None, "row"),
        ),
        check_vma=False,
    )
```

```python
import functools

import jax
import jax.numpy as jnp
from jax import lax
from jax.experimental import pallas as pl
from jax.experimental.pallas import tpu as pltpu
from jax.sharding import PartitionSpec as P

F32 = jnp.float32
BF16 = jnp.bfloat16
GROUPS = (5, 5, 4)
TILE = 256
SCALE = 1000000000
VMEM = pl.BlockSpec(memory_space=pltpu.VMEM)
ANY = pl.BlockSpec(memory_space=pl.ANY)
MINE = (0, 1, 3, 5, 7)
LENT = (2, 4, 6)


def around(value):
    perm = []
    for dp in range(4):
        step = 1 if dp % 2 == 0 else -1
        for z in range(8):
            perm.append((dp * 8 + z, dp * 8 + (z + step) % 8))
    return lax.ppermute(value, ("dp", "col"), perm)


def swap_core(value):
    return lax.ppermute(value, "dp", [(i, i ^ 1) for i in range(4)])


def swap_chip(value):
    return lax.ppermute(value, "dp", [(i, i ^ 2) for i in range(4)])


def swap_pair(value):
    return lax.ppermute(value, "row", [(i, i ^ 4) for i in range(8)])


def along_y(value, step):
    return lax.ppermute(
        value, "row", [(i, (i // 4) * 4 + (i % 4 + step) % 4) for i in range(8)]
    )


def place():
    col = lax.axis_index("col")
    sign = 1 - 2 * lax.rem(lax.axis_index("dp"), 2)
    return col, sign


def wrap(v, n=8):
    return lax.rem(v + 8 * n, n)


class Order:
    def __init__(self):
        self.before = ()

    def __call__(self, kernel, outs, ins, scratch=(), limit=None, alias=None, work=0.3):
        count, waits = len(ins), len(self.before)

        def body(*refs):
            kernel(*refs[:count], *refs[count + waits :])

        got = pl.pallas_call(
            body,
            out_shape=[make(shape, dtype) for make, shape, dtype, _ in outs],
            in_specs=[spec for _, spec in ins] + [ANY] * waits,
            out_specs=[spec for _, _, _, spec in outs],
            scratch_shapes=list(scratch),
            input_output_aliases=alias or {},
            compiler_params=pltpu.CompilerParams(vmem_limit_bytes=limit),
            cost_estimate=pl.CostEstimate(
                flops=int(work * SCALE), bytes_accessed=1, transcendentals=0
            ),
        )(*[a for a, _ in ins], *self.before)
        self.before = (got[-1],)
        return got


def mm(a, b):
    return jnp.dot(a, b, preferred_element_type=F32)


def grads_of(gate, up, flow, out):
    size = gate.shape[1]
    gate_value = gate.astype(F32)
    logistic = jax.nn.sigmoid(gate_value)
    weighted = flow.astype(F32) * logistic
    out[:, size:] = (weighted * gate_value).astype(BF16)
    out[:, :size] = (
        weighted * up.astype(F32) * (1.0 + gate_value * (1.0 - logistic))
    ).astype(BF16)


def grads_kernel(bounds, gate_any, up_any, flow_any, *refs):
    outs = refs[: len(bounds)]
    gate, up, flow, sems = refs[len(bounds) :]
    copies = []
    for k, (lo, hi) in enumerate(bounds):
        columns = pl.ds(lo, hi - lo)
        copies.append(
            [
                pltpu.make_async_copy(source.at[:, columns], target.at[:, columns], sems.at[k, i])
                for i, (source, target) in enumerate(
                    ((gate_any, gate), (up_any, up), (flow_any, flow))
                )
            ]
        )
        for copy in copies[k]:
            copy.start()
    for k, (lo, hi) in enumerate(bounds):
        for copy in copies[k]:
            copy.wait()
        grads_of(gate[:, lo:hi], up[:, lo:hi], flow[:, lo:hi], outs[k])


def join_kernel(a, b, out):
    n = a.shape[0]
    out[:n] = a[...]
    out[n:] = b[...]


def near_block(near, ident):
    row = lax.axis_index("row")
    k = wrap(ident - row, 4)
    return near[k, lax.rem(ident // 4 + row // 4, 2)]


def lend_tokens_kernel(own, above, far, below, out0, out1, out2, near):
    col, sign = place()
    for i, ref in enumerate((own, above, far, below)):
        near[i] = ref[...]
    for i, out in enumerate((out0, out1, out2)):
        out[...] = near_block(near, wrap(col - sign * (7 - i)))


def tokens_kernel(near, got0, got1, got2, out, laid):
    col, sign = place()
    rows, width = near.shape[2:]
    slab = width // 4
    for s, at in enumerate(MINE):
        laid[at * rows : (at + 1) * rows] = near_block(near, wrap(col - sign * s))
    for got, at in zip((got0, got1, got2), LENT):
        laid[at * rows : (at + 1) * rows] = got[...]
    for i, flip in enumerate((0, 2, 1, 3)):
        q = lax.axis_index("dp") ^ flip
        columns = pl.ds(pl.multiple_of(q * slab, slab), slab)
        for t in range(0, 8 * rows, TILE):
            out[i * slab : (i + 1) * slab, t : t + TILE] = laid[t : t + TILE, columns].T


def lay(pieces, cat):
    at = 0
    for piece in pieces:
        cat[at : at + piece.shape[0]] = piece[...]
        at += piece.shape[0]


def weight_kernel(own, first, second, third, last, xt, cat, *outs):
    lay((own, first, second, third, last), cat)
    @pl.loop(0, cat.shape[1] // TILE)
    def _(t):
        columns = pl.ds(pl.multiple_of(t * TILE, TILE), TILE)
        total = mm(xt[...], cat[:, columns])
        at = 0
        for out in outs:
            n = out.shape[0]
            out[:, columns] = total[at : at + n].astype(out.dtype)
            at += n


def pair_kernel(keep, got0, got1, far):
    half = got0.shape[0]
    far[:half] = (keep[:half] + got0[...].astype(F32)).astype(BF16)
    far[half:] = (keep[half:] + got1[...].astype(F32)).astype(BF16)


def score_kernel(lo, aliased, near, got, far, w_gate, w_up, *refs):
    out_gate, out_up, mark, slab_gate, slab_up, res_gate, res_up, sems = refs[2 if aliased else 0 :]
    mark[...] = jnp.zeros_like(mark)
    replica = lax.axis_index("dp")
    slab, size = slab_gate.shape
    rows = pl.ds(pl.multiple_of(replica * slab, slab), slab)
    read = [
        pltpu.make_async_copy(w.at[rows, pl.ds(lo, size)], target, sems.at[i])
        for i, (w, target) in enumerate(((w_gate, slab_gate), (w_up, slab_up)))
    ]
    write = [
        pltpu.make_async_copy(value, out.at[:, pl.ds(lo, size)], sems.at[2 + i])
        for i, (value, out) in enumerate(((res_gate, out_gate), (res_up, out_up)))
    ]
    for copy in read:
        copy.start()
    for i, (w, value) in enumerate(((slab_gate, res_gate), (slab_up, res_up))):
        read[i].wait()
        columns = slice(i * size, (i + 1) * size)
        total = near[:, columns] + got[:, columns].astype(F32) + far[:, columns].astype(F32)
        value[...] = -w[...].astype(F32) * total
        write[i].start()
    for copy in write:
        copy.wait()


def turn_kernel(lo, w_gate, w_up, out, held, sems):
    size = out.shape[0] // 2
    copies = [
        pltpu.make_async_copy(w.at[:, pl.ds(lo, size)], held.at[i], sems.at[i])
        for i, w in enumerate((w_gate, w_up))
    ]
    for copy in copies:
        copy.start()
    for i, copy in enumerate(copies):
        copy.wait()
        for t in range(0, size, 128):
            out[i * size + t : i * size + t + 128, :] = held[i, :, t : t + 128].T


def tokens_part_kernel(cat, turned, out):
    @pl.loop(0, out.shape[1] // TILE)
    def _(t):
        columns = pl.ds(pl.multiple_of(t * TILE, TILE), TILE)
        out[:, columns] = mm(cat[...], turned[:, columns])


def tokens_last_kernel(*refs):
    unit1, unit2 = refs[:5], refs[5:10]
    part, turned1, turned2, mine, lend0, lend1, lend2, cat1, cat2 = refs[10:]
    r = unit1[0].shape[0]
    lay(unit1, cat1)
    lay(unit2, cat2)
    for t in range(0, turned1.shape[1], TILE):
        columns = slice(t, t + TILE)
        total = mm(cat1[...], turned1[:, columns]) + part[:, columns]
        total = total + mm(cat2[...], turned2[:, columns])
        for i, p in enumerate(MINE):
            mine[i * r : (i + 1) * r, columns] = total[p * r : (p + 1) * r].astype(BF16)
        for out, p in zip((lend0, lend1, lend2), LENT):
            out[:, columns] = total[p * r : (p + 1) * r].astype(BF16)


def spread_kernel(mine, back0, back1, back2, *refs):
    outs, every = refs[:-1], refs[-1]
    col, sign = place()
    row = lax.axis_index("row")
    r = every.shape[2]
    blocks = [(s, mine, s) for s in range(5)] + [(7, back0, 0), (6, back1, 0), (5, back2, 0)]
    for s, ref, i in blocks:
        ident = wrap(col - sign * s)
        every[wrap(ident - row, 4), lax.rem(ident // 4 + row // 4, 2)] = ref[i * r : (i + 1) * r]
    for i, out in enumerate(outs):
        out[...] = every[i]


def sum_y_kernel(hold, a, b, c, own, send):
    def total(j):
        return (hold[j].astype(F32) + a[j].astype(F32)) + (b[j].astype(F32) + c[j].astype(F32))

    own[...] = total(0)
    send[...] = total(1).astype(BF16)


def last_kernel(own, got, out, mark):
    mark[...] = jnp.zeros_like(mark)
    out[...] = (own[...] + got[...].astype(F32)).astype(BF16)


def relay_kernel(*refs):
    pass


def shards(tokens, gate_pre, up_pre, d_hidden, w_gate, w_up):
    rows, width = tokens.shape
    hidden = gate_pre.shape[1]
    slab = width // 4
    many = 8 * rows
    mib = 1 << 20
    bounds, at = [], 0
    for parts in GROUPS:
        size = hidden * parts // sum(GROUPS)
        bounds.append((at, at + size))
        at += size

    run = Order()
    some = jax.ShapeDtypeStruct

    def fixed(*arrays):
        return [(pltpu.with_memory_space_constraint(a, pltpu.HBM), ANY) for a in arrays]

    weights = fixed(w_gate, w_up)

    def v(*arrays):
        return [(a, VMEM) for a in arrays]

    def one(kernel, shape, dtype, arrays, limit, scratch=()):
        return run(kernel, [(some, shape, dtype, VMEM)], v(*arrays), scratch, limit * mib)[0]

    def join(a, b):
        return one(join_kernel, (2 * a.shape[0],) + a.shape[1:], BF16, (a, b), 3)

    def relay(*values):
        return run(
            relay_kernel,
            [(some, value.shape, value.dtype, ANY) for value in values],
            [(value, ANY) for value in values],
            limit=mib,
            alias={i: i for i in range(len(values))},
        )

    def turn(bound):
        size = bound[1] - bound[0]
        return run(
            functools.partial(turn_kernel, bound[0]),
            [(some, (2 * size, width), BF16, VMEM)],
            weights,
            [pltpu.VMEM((2, width, size), BF16), pltpu.SemaphoreType.DMA((2,))],
            9 * mib,
            work=3,
        )[0]

    def weight_grads(pieces):
        cols = pieces[0].shape[1]
        outs = [(some, (many, cols), BF16, VMEM)]
        outs += [(some, (slab, cols), dtype, VMEM) for dtype in (F32, F32, BF16)]
        outs += [(some, (slab // 2, cols), BF16, VMEM)] * 2
        cat, near, far, send_near, *send_far = run(
            weight_kernel, outs, v(*pieces, xt), limit=19 * mib, work=0.5
        )
        return cat, (near, swap_core(send_near)), (far, *[swap_core(part) for part in send_far])

    def pair_sum(parts):
        return swap_chip(one(pair_kernel, parts[0].shape, BF16, parts, 6))

    def scores(near, far, bound, before):
        near, got = near
        lo, hi = bound
        size = hi - lo
        scratch = (
            [pltpu.VMEM((slab, size), BF16)] * 2
            + [pltpu.VMEM((slab, size), F32)] * 2
            + [pltpu.SemaphoreType.DMA((4,))]
        )
        return run(
            functools.partial(score_kernel, lo, bool(before)),
            [(pltpu.HBM, (slab, hidden), F32, ANY)] * 2 + [(some, (8, 128), F32, VMEM)],
            v(near, got, far) + weights + fixed(*before),
            scratch,
            8 * mib,
            {5: 0, 6: 1} if before else None,
        )[:2]

    def tokens_last(unit1, unit2, part):
        outs = [(some, (5 * rows, width), BF16, VMEM)] + [(some, (rows, width), BF16, VMEM)] * 3
        mine, *lend = run(
            tokens_last_kernel,
            outs,
            v(*unit1, *unit2, part, turned1, turned2),
            [pltpu.VMEM((many, unit[0].shape[1]), BF16) for unit in (unit1, unit2)],
            27 * mib,
            work=1,
        )
        return mine, [swap_core(block) for block in lend]

    def tokens_part(cat, turned):
        return one(tokens_part_kernel, (many, width), F32, (cat, turned), 18)

    def spread(mine, back):
        hold, up, far, down = run(
            spread_kernel,
            [(some, (2, rows, width), BF16, VMEM)] * 4,
            v(mine, *back),
            [pltpu.VMEM((4, 2, rows, width), BF16)],
            limit=8 * mib,
        )
        return hold, along_y(up, 1), along_y(far, 2), along_y(down, -1)

    def sum_y(parts):
        r = parts[0].shape[1]
        outs = [(some, (r, width), F32, VMEM), (some, (r, width), BF16, VMEM)]
        own, send = run(sum_y_kernel, outs, v(*parts), limit=4 * mib)
        return own, swap_pair(send)

    sizes = [2 * (hi - lo) for lo, hi in bounds]
    g0, g1, g2 = run(
        functools.partial(grads_kernel, bounds),
        [(some, (rows, size), BF16, VMEM) for size in sizes],
        fixed(gate_pre, up_pre, d_hidden),
        [pltpu.VMEM((rows, hidden), BF16)] * 3 + [pltpu.SemaphoreType.DMA((len(bounds), 3))],
        limit=5 * mib,
    )
    a1 = around(join(g0, swap_core(g0)))
    b1 = around(join(g1, swap_core(g1)))
    c0 = join(g2, swap_core(g2))
    turned0 = turn(bounds[0])
    a1, c0 = relay(a1, c0)
    a2, c1 = around(a1), around(c0)
    both = join(tokens[None], swap_pair(tokens)[None])
    above, below = along_y(both, -1), along_y(both, 1)
    b1 = relay(b1)[0]
    b2 = around(b1)
    turned1 = turn(bounds[1])
    a2 = relay(a2)[0]
    a3 = around(a2)
    c1 = relay(c1)[0]
    c2 = around(c1)
    b2, above, below = relay(b2, above, below)
    b3 = around(b2)
    far = along_y(both, 2)
    turned2 = turn(bounds[2])
    a3 = relay(a3)[0]
    a4 = around(a3[:rows])
    c2 = relay(c2)[0]
    c3 = around(c2)
    b3, far = relay(b3, far)
    b4 = around(b3[:rows])
    *lend, near = run(
        lend_tokens_kernel,
        [(some, (rows, width), BF16, VMEM)] * 3 + [(some, (4, 2, rows, width), BF16, VMEM)],
        v(both, above, far, below),
        limit=8 * mib,
    )
    lent = [swap_core(block) for block in lend]
    a4 = relay(a4)[0]
    xt = one(
        tokens_kernel,
        (width, many),
        BF16,
        (near, *lent),
        11,
        [pltpu.VMEM((many, width), BF16)],
    )
    cat0, near0, far0 = weight_grads((g0, a1, a2, a3, a4))
    c3 = relay(c3)[0]
    c4 = around(c3[:rows])
    far0 = pair_sum(far0)
    part = tokens_part(cat0, turned0)
    b4 = relay(b4)[0]
    c4 = relay(c4)[0]
    unit1, unit2 = (g1, b1, b2, b3, b4), (g2, c1, c2, c3, c4)
    mine, back = tokens_last(unit1, unit2, part)
    _, near1, far1 = weight_grads(unit1)
    parts = spread(mine, back)
    far1 = pair_sum(far1)
    far0 = relay(far0)[0]
    _, near2, far2 = weight_grads(unit2)
    far2 = pair_sum(far2)
    done = scores(near0, far0, bounds[0], ())
    done = scores(near1, far1, bounds[1], done)
    own, got = sum_y(parts)
    outs = [(some, (rows, width), BF16, VMEM), (some, (8, 128), F32, VMEM)]
    d_tokens = run(last_kernel, outs, v(own, got), limit=4 * mib)[0]
    done = scores(near2, far2, bounds[2], done)
    score_gate, score_up = [d.reshape(1, 1, slab, hidden) for d in done]
    return (d_tokens, score_gate, score_up)


def solution(mesh):
    placed = (
        P(("dp", "row"), "col"),
        P(("dp", "col"), "row"),
        P(("dp", "col"), "row"),
        P(("dp", "col"), "row"),
        P("col", "row"),
        P("col", "row"),
    )
    return jax.shard_map(
        shards,
        mesh=mesh,
        in_specs=placed,
        out_specs=(
            P(("dp", "row"), "col"),
            P("col", "dp", None, "row"),
            P("col", "dp", None, "row"),
        ),
        check_vma=False,
    )
```
